512 devices in a mesh: dp: 4 (over z_lo), seq: 128 (over x, z_hi, y, core).
Axes of the slice: x: 4, y: 4, z: 16 (z_hi: 4, z_lo: 4; z = z_hi * 4 + z_lo), core: 2. Of those that a mesh axis runs over, the one named last changes fastest.
Arguments:
- tokens: bfloat16 [4, 32768, 2048], P('dp', 'seq'), may hold values from -6 to 6
- cotangent: bfloat16 [4, 32768, 2048], P('dp', 'seq'), may hold values from -6 to 6
- kernel: bfloat16 [32768, 2048], P('seq'), may hold values from -6 to 6
- first_factor: bfloat16 [128, 256, 256], P('seq'), may hold values from -0.375 to 0.375
- second_factor: bfloat16 [256, 128, 128], P('seq'), may hold values from -0.5 to 0.5
Outputs:
- grad_kernel: bfloat16 [32768, 2048], P('seq')
- grad_first: float32 [128, 256, 256], P('seq')
- grad_second: float32 [256, 128, 128], P('seq')
The draws below stay inside these ranges and needn't reach their ends.
All inputs are finite; a program needn't handle non-finite values.
Results may differ from the reference program's by a relative error of at most 0.0058.
Values may be sent and summed in bfloat16 or wider, within the bound.
No kernel may reach another device: no remote copies, remote signals or barrier semaphores. Data moves between devices by JAX's collectives and lax.ppermute only.
A program may use at most 64 MiB of HBM per device.

```python
import math
import jax
import jax.numpy as jnp
from jax import lax

D = 2048
GB = 256
SEQS = 4
L = 32768
GA = 128


def levels(rng, extent, cuts, smallest, largest):
    gain = 1.0
    for dim, blocks in cuts:
        heights = jax.random.uniform(jax.random.fold_in(jax.random.fold_in(rng, 6), dim), (blocks,), jnp.float32, smallest / len(cuts), largest / len(cuts))
        gain = gain * jnp.repeat(jnp.exp(heights), extent[dim] // blocks).reshape((-1,) + (1,) * (len(extent) - 1 - dim))
    return gain


def normal_values(stream_key, dims, scale, bound, pieces=(), held_as=jnp.bfloat16):
    entries = scale * jax.random.normal(stream_key, dims, jnp.float32)
    if pieces:
        entries = entries * levels(stream_key, dims, pieces, -0.22, 0.18)
    return jnp.clip(entries, -bound, bound).astype(held_as)


def setup_inputs(seed: int = 0) -> dict:
    streams_of = jax.random.split(jax.random.key(seed), 6)
    tokens = normal_values(streams_of[0], (SEQS, L, D), 1.0, 6.0, ((0, 4), (1, 128)))
    cotangent = normal_values(streams_of[1], (SEQS, L, D), 1.0, 6.0, ((0, 4), (1, 128)))
    kernel = normal_values(streams_of[2], (L, D), 1.0, 6.0, ((0, 128),))
    first_factor = normal_values(streams_of[3], (GA, GB, GB), GB ** -0.5, 0.375, ((0, 128),))
    second_factor = normal_values(streams_of[4], (GB, GA, GA), GA ** -0.5, 0.5, ((0, 128),))
    return dict(tokens=tokens, cotangent=cotangent, kernel=kernel, first_factor=first_factor, second_factor=second_factor)


def rounded(values):
    return lax.optimization_barrier(values.astype(jnp.bfloat16)).astype(jnp.float32)

def product(spec, left, right):
    return jnp.einsum(spec, left, right)

def reference(tokens, cotangent, kernel, first_factor, second_factor):
    block_width = min(D, 256)
    natural_all = tokens.reshape(SEQS, GA, GB, D)
    upstream_all = cotangent.reshape(SEQS, GA, GB, D)
    kernel_all = kernel.reshape(GB, GA, D)
    first_mat = first_factor.astype(jnp.float32)
    second_mat = second_factor.astype(jnp.float32)

    def over_channels(totals, offset):
        first_grad, second_grad = totals
        kernel_part = lax.dynamic_slice_in_dim(kernel_all, offset, block_width, 2).astype(jnp.float32)
        kernel_grad = jnp.zeros((GB, GA, block_width), jnp.float32)
        for member in range(SEQS):
            natural = lax.dynamic_slice_in_dim(natural_all[member], offset, block_width, 2).astype(jnp.float32)
            upstream = lax.dynamic_slice_in_dim(upstream_all[member], offset, block_width, 2).astype(jnp.float32)
            mixed_in = rounded(product('aqb,abc->aqc', first_mat, natural))
            mixed_up = rounded(product('aqb,abc->aqc', first_mat, upstream))
            forward = product('bpa,abc->bpc', second_mat, mixed_in)
            backward = product('bpa,abc->bpc', second_mat, mixed_up)
            kernel_grad = kernel_grad + forward * backward
            weighted = rounded(kernel_part * forward)
            pulled = rounded(kernel_part * backward)
            second_grad = second_grad + product('bpc,abc->bpa', pulled, mixed_in) + product('bpc,abc->bpa', weighted, mixed_up)
            spread = rounded(product('bpa,bpc->abc', second_mat, weighted))
            pulled_back = rounded(product('bpa,bpc->abc', second_mat, pulled))
            first_grad = first_grad + product('aqc,abc->aqb', pulled_back, natural) + product('aqc,abc->aqb', spread, upstream)
        return ((first_grad, second_grad), kernel_grad)
    initial = (jnp.zeros((GA, GB, GB), jnp.float32), jnp.zeros((GB, GA, GA), jnp.float32))
    offsets = jnp.arange(D // block_width, dtype=jnp.int32) * block_width
    totals, kernel_blocks = lax.scan(over_channels, initial, offsets)
    kernel_total = jnp.moveaxis(kernel_blocks, 0, 2).reshape(L, D)
    seq_share = 1.0 / math.sqrt(SEQS)
    factor_share = 1.0 / math.sqrt(2.0 * D * SEQS)
    grad_kernel = (kernel_total * seq_share).astype(jnp.bfloat16)
    return (grad_kernel, totals[0] * factor_share, totals[1] * factor_share)
```

```python
import math

import jax
import jax.numpy as jnp
from jax import lax
from jax.experimental import pallas as pl
from jax.experimental.pallas import tpu as pltpu
from jax.sharding import PartitionSpec as P

LANES = 128


def nn(left, right):
    return lax.dot_general(left, right, (((1,), (0,)), ((), ())), preferred_element_type=jnp.float32)


def nt(left, right):
    return lax.dot_general(left, right, (((1,), (1,)), ((), ())), preferred_element_type=jnp.float32)


def tn(left, right):
    return lax.dot_general(left, right, (((0,), (0,)), ((), ())), preferred_element_type=jnp.float32)


def mix_kernel(own, cols, first_ref, tokens_ref, cotangent_ref, out_ref, rows_ref, factor_ref):
    groups, rows, _ = out_ref.shape

    @pl.when(pl.program_id(0) == 0)
    def _():
        for h in range(factor_ref.shape[0]):
            factor_ref[h] = first_ref[0, :, h * LANES : (h + 1) * LANES].astype(jnp.float32)

    for q in range(own):
        factor = jnp.concatenate(
            [
                factor_ref[h, pl.ds(q, groups, stride=own), :].astype(jnp.bfloat16)
                for h in range(factor_ref.shape[0])
            ],
            axis=1,
        )
        for t, ref in enumerate((tokens_ref, cotangent_ref)):
            mixed = nn(factor, ref[0])
            for ci in range(cols):
                rows_ref[pl.ds((t * cols + ci) * own + q, groups, stride=rows), :] = mixed[
                    :, ci * LANES : (ci + 1) * LANES
                ]
    out_ref[...] = rows_ref[...].reshape(groups, rows, LANES).astype(jnp.bfloat16)


def middle_kernel(
    own, cols, shares, arrived_ref, kernel_ref, second_ref, back_ref, kernel_out_ref, second_out_ref, rows_ref, total_ref
):
    _, groups, rows, _ = arrived_ref.shape
    step = pl.program_id(0)
    last = pl.num_programs(0) - 1
    seq_share, factor_share = shares

    @pl.when(step == 0)
    def _():
        total_ref[...] = jnp.zeros_like(total_ref)
        second_out_ref[...] = jnp.zeros_like(second_out_ref)

    rows_ref[...] = arrived_ref[0].astype(jnp.float32).reshape(groups * rows, LANES)
    for q in range(own):
        factor = second_ref[q]
        held = []
        for t in range(2):
            held.append(
                jnp.concatenate(
                    [
                        rows_ref[pl.ds((t * cols + ci) * own + q, groups, stride=rows), :].astype(jnp.bfloat16)
                        for ci in range(cols)
                    ],
                    axis=1,
                )
            )
        mixed_in, mixed_up = held
        forward = nn(factor, mixed_in)
        backward = nn(factor, mixed_up)
        points = factor.shape[0]
        scale = kernel_ref[q * points : (q + 1) * points, :].astype(jnp.float32)
        total_ref[q] += forward * backward
        weighted = (scale * forward).astype(jnp.bfloat16)
        pulled = (scale * backward).astype(jnp.bfloat16)
        second_out_ref[q] += (nt(pulled, mixed_in) + nt(weighted, mixed_up)) * factor_share
        for t, values in enumerate((weighted, pulled)):
            spread = tn(factor, values)
            for ci in range(cols):
                rows_ref[pl.ds((t * cols + ci) * own + q, groups, stride=rows), :] = spread[
                    :, ci * LANES : (ci + 1) * LANES
                ]
    back_ref[0] = rows_ref[...].reshape(groups, rows, LANES).astype(jnp.bfloat16)

    @pl.when(step == last)
    def _():
        own_points = total_ref.shape[0] * total_ref.shape[1]
        kernel_out_ref[...] = (total_ref[...] * seq_share).astype(jnp.bfloat16).reshape(own_points, -1)


def final_kernel(own, cols, factor_share, returned_ref, tokens_ref, cotangent_ref, out_ref, rows_ref, total_ref):
    groups, rows, _ = returned_ref.shape
    step = pl.program_id(0)
    last = pl.num_programs(0) - 1

    @pl.when(step == 0)
    def _():
        total_ref[...] = jnp.zeros_like(total_ref)

    rows_ref[...] = returned_ref[...].astype(jnp.float32).reshape(groups * rows, LANES)
    for q in range(own):
        held = []
        for t in range(2):
            held.append(
                jnp.concatenate(
                    [
                        rows_ref[pl.ds((t * cols + ci) * own + q, groups, stride=rows), :].astype(jnp.bfloat16)
                        for ci in range(cols)
                    ],
                    axis=1,
                )
            )
        spread, pulled_back = held
        part = nt(pulled_back, tokens_ref[0]) + nt(spread, cotangent_ref[0])
        for h in range(total_ref.shape[0]):
            total_ref[h, pl.ds(q, groups, stride=own), :] += part[:, h * LANES : (h + 1) * LANES]

    @pl.when(step == last)
    def _():
        for h in range(total_ref.shape[0]):
            out_ref[:, h * LANES : (h + 1) * LANES] = total_ref[h] * factor_share


def shards(tokens, cotangent, kernel, first_factor, second_factor):
    ranks, members = lax.axis_size("dp"), lax.axis_size("seq")
    _, local_rows, channels = tokens.shape
    own, points, _ = second_factor.shape
    share = channels // ranks
    cols = share // LANES
    rows = 2 * cols * own
    groups = local_rows // own
    seq_share = 1.0 / math.sqrt(ranks)
    factor_share = 1.0 / math.sqrt(2.0 * channels * ranks)
    both = pl.BlockSpec((1, local_rows, share), lambda k: (0, 0, k))
    message = jax.ShapeDtypeStruct((ranks * members, rows, LANES), jnp.bfloat16)
    params = pltpu.CompilerParams(dimension_semantics=("arbitrary",), vmem_limit_bytes=40 * 1024 * 1024)
    row_scratch = pltpu.VMEM((groups * rows, LANES), jnp.float32)

    with jax.named_scope("mix"):
        mixed = pl.pallas_call(
            lambda *refs: mix_kernel(own, cols, *refs),
            out_shape=message,
            grid=(ranks,),
            in_specs=[pl.BlockSpec((1, local_rows, local_rows), lambda k: (0, 0, 0)), both, both],
            out_specs=pl.BlockSpec((members, rows, LANES), lambda k: (k, 0, 0)),
            scratch_shapes=[row_scratch, pltpu.VMEM((local_rows // LANES, local_rows, LANES), jnp.float32)],
            compiler_params=params,
            name="mix",
        )(first_factor, tokens, cotangent)
    with jax.named_scope("send"):
        arrived = lax.all_to_all(mixed, ("dp", "seq"), split_axis=0, concat_axis=0, tiled=True)
    quarter = lax.dynamic_slice_in_dim(kernel, lax.axis_index("dp") * share, share, 1)
    with jax.named_scope("middle"):
        back, kernel_part, second_part = pl.pallas_call(
            lambda *refs: middle_kernel(own, cols, (seq_share, factor_share), *refs),
            out_shape=(
                jax.ShapeDtypeStruct((ranks, members, rows, LANES), jnp.bfloat16),
                jax.ShapeDtypeStruct((own * points, share), jnp.bfloat16),
                jax.ShapeDtypeStruct((own, points, members), jnp.float32),
            ),
            grid=(ranks,),
            in_specs=[
                pl.BlockSpec((1, members, rows, LANES), lambda s: (s, 0, 0, 0)),
                pl.BlockSpec((own * points, share), lambda s: (0, 0)),
                pl.BlockSpec((own, points, members), lambda s: (0, 0, 0)),
            ],
            out_specs=(
                pl.BlockSpec((1, members, rows, LANES), lambda s: (s, 0, 0, 0)),
                pl.BlockSpec((own * points, share), lambda s: (0, 0)),
                pl.BlockSpec((own, points, members), lambda s: (0, 0, 0)),
            ),
            scratch_shapes=[row_scratch, pltpu.VMEM((own, points, share), jnp.float32)],
            compiler_params=params,
            name="middle",
        )(arrived.reshape(ranks, members, rows, LANES), quarter, second_factor)
    with jax.named_scope("gather_kernel"):
        kernel_out = lax.all_gather(kernel_part, "dp", axis=1, tiled=True)
    with jax.named_scope("return"):
        returned = lax.all_to_all(
            back.reshape(ranks * members, rows, LANES), ("dp", "seq"), split_axis=0, concat_axis=0, tiled=True
        )
    with jax.named_scope("final"):
        first_part = pl.pallas_call(
            lambda *refs: final_kernel(own, cols, factor_share, *refs),
            out_shape=jax.ShapeDtypeStruct((local_rows, local_rows), jnp.float32),
            grid=(ranks,),
            in_specs=[pl.BlockSpec((members, rows, LANES), lambda k: (k, 0, 0)), both, both],
            out_specs=pl.BlockSpec((local_rows, local_rows), lambda k: (0, 0)),
            scratch_shapes=[row_scratch, pltpu.VMEM((local_rows // LANES, local_rows, LANES), jnp.float32)],
            compiler_params=params,
            name="final",
        )(returned, tokens, cotangent)
    with jax.named_scope("sum"):
        first_total, second_total = lax.psum((first_part, second_part), "dp")
    return kernel_out, first_total[None], second_total


def solution(mesh):
    in_specs = (
        P("dp", "seq", None),
        P("dp", "seq", None),
        P("seq", None),
        P("seq", None, None),
        P("seq", None, None),
    )
    out_specs = (P("seq", None), P("seq", None, None), P("seq", None, None))
    return jax.shard_map(shards, mesh=mesh, in_specs=in_specs, out_specs=out_specs, check_vma=False)
```

```python
import math

import jax
import jax.numpy as jnp
from jax import lax
from jax.experimental import pallas as pl
from jax.experimental.pallas import tpu as pltpu
from jax.sharding import PartitionSpec as P

LANES = 128


def nn(left, right):
    return lax.dot_general(left, right, (((1,), (0,)), ((), ())), preferred_element_type=jnp.float32)


def nt(left, right):
    return lax.dot_general(left, right, (((1,), (1,)), ((), ())), preferred_element_type=jnp.float32)


def tn(left, right):
    return lax.dot_general(left, right, (((0,), (0,)), ((), ())), preferred_element_type=jnp.float32)


def mix_kernel(own, cols, first_ref, tokens_ref, cotangent_ref, out_ref, rows_ref, factor_ref):
    groups, rows, _ = out_ref.shape

    @pl.when(pl.program_id(0) == 0)
    def _():
        for h in range(factor_ref.shape[0]):
            factor_ref[h] = first_ref[0, :, h * LANES : (h + 1) * LANES].astype(jnp.float32)

    for q in range(own):
        factor = jnp.concatenate(
            [
                factor_ref[h, pl.ds(q, groups, stride=own), :].astype(jnp.bfloat16)
                for h in range(factor_ref.shape[0])
            ],
            axis=1,
        )
        for t, ref in enumerate((tokens_ref, cotangent_ref)):
            mixed = nn(factor, ref[0])
            for ci in range(cols):
                rows_ref[pl.ds((t * cols + ci) * own + q, groups, stride=rows), :] = mixed[
                    :, ci * LANES : (ci + 1) * LANES
                ]
    out_ref[...] = rows_ref[...].reshape(groups, rows, LANES).astype(jnp.bfloat16)


def pack(blocks_ref, part_ref, start):
    own, points, _ = blocks_ref.shape
    fold = part_ref.shape[1] // LANES
    height = points // fold
    for q in range(own):
        for f in range(fold):
            part_ref[start + q * height : start + (q + 1) * height, f * LANES : (f + 1) * LANES] = blocks_ref[
                q, f * height : (f + 1) * height, :
            ].astype(jnp.bfloat16)


def middle_kernel(
    own, cols, shares, arrived_ref, kernel_ref, second_ref, back_ref, part_ref, rows_ref, total_ref, second_ref_total
):
    _, groups, rows, _ = arrived_ref.shape
    step = pl.program_id(0)
    last = pl.num_programs(0) - 1
    seq_share, factor_share = shares

    @pl.when(step == 0)
    def _():
        total_ref[...] = jnp.zeros_like(total_ref)
        second_ref_total[...] = jnp.zeros_like(second_ref_total)

    rows_ref[...] = arrived_ref[0].astype(jnp.float32).reshape(groups * rows, LANES)
    for q in range(own):
        factor = second_ref[q]
        held = []
        for t in range(2):
            held.append(
                jnp.concatenate(
                    [
                        rows_ref[pl.ds((t * cols + ci) * own + q, groups, stride=rows), :].astype(jnp.bfloat16)
                        for ci in range(cols)
                    ],
                    axis=1,
                )
            )
        mixed_in, mixed_up = held
        forward = nn(factor, mixed_in)
        backward = nn(factor, mixed_up)
        points = factor.shape[0]
        scale = kernel_ref[q * points : (q + 1) * points, :].astype(jnp.float32)
        total_ref[q] += forward * backward
        weighted = (scale * forward).astype(jnp.bfloat16)
        pulled = (scale * backward).astype(jnp.bfloat16)
        second_ref_total[q] += (nt(pulled, mixed_in) + nt(weighted, mixed_up)) * factor_share
        for t, values in enumerate((weighted, pulled)):
            spread = tn(factor, values)
            for ci in range(cols):
                rows_ref[pl.ds((t * cols + ci) * own + q, groups, stride=rows), :] = spread[
                    :, ci * LANES : (ci + 1) * LANES
                ]
    back_ref[0] = rows_ref[...].reshape(groups, rows, LANES).astype(jnp.bfloat16)

    @pl.when(step == last)
    def _():
        points = total_ref.shape[1]
        for q in range(own):
            part_ref[q * points : (q + 1) * points, :] = (total_ref[q] * seq_share).astype(jnp.bfloat16)
        pack(second_ref_total, part_ref, own * points)


def final_kernel(
    own, cols, ranks, factor_share, returned_ref, tokens_ref, cotangent_ref, out_ref, rows_ref, total_ref, held_ref, sems
):
    groups, rows, _ = returned_ref.shape
    share = cols * LANES
    step = pl.program_id(0)
    last = pl.num_programs(0) - 1

    def loads(k):
        chunk = pl.ds(pl.multiple_of(k * share, share), share)
        return [
            pltpu.make_async_copy(ref.at[0, :, chunk], held_ref.at[t, k], sems.at[t, k])
            for t, ref in enumerate((tokens_ref, cotangent_ref))
        ]

    @pl.when(step == 0)
    def _():
        for k in range(ranks):
            for copy in loads(k):
                copy.start()
        total_ref[...] = jnp.zeros_like(total_ref)

    rows_ref[...] = returned_ref[...].astype(jnp.float32).reshape(groups * rows, LANES)
    for copy in loads(step):
        copy.wait()
    for q in range(own):
        held = []
        for t in range(2):
            held.append(
                jnp.concatenate(
                    [
                        rows_ref[pl.ds((t * cols + ci) * own + q, groups, stride=rows), :].astype(jnp.bfloat16)
                        for ci in range(cols)
                    ],
                    axis=1,
                )
            )
        spread, pulled_back = held
        part = nt(pulled_back, held_ref[0, step]) + nt(spread, held_ref[1, step])
        for h in range(total_ref.shape[0]):
            total_ref[h, pl.ds(q, groups, stride=own), :] += part[:, h * LANES : (h + 1) * LANES]

    @pl.when(step == last)
    def _():
        for h in range(total_ref.shape[0]):
            out_ref[:, h * LANES : (h + 1) * LANES] = (total_ref[h] * factor_share).astype(jnp.bfloat16)


def join_kernel(ranks, *refs):
    firsts_ref, pieces, outs = refs[0], refs[1 : 1 + ranks], refs[1 + ranks :]
    kernel_out_ref, first_out_ref, second_out_ref = outs
    own, points, _ = second_out_ref.shape
    share = pieces[0].shape[1]
    me = lax.axis_index("dp")
    for r in range(ranks):
        chunk = pl.ds(pl.multiple_of(lax.rem(me + ranks - r, ranks) * share, share), share)
        kernel_out_ref[:, chunk] = pieces[r][: own * points, :]
    first = firsts_ref[0].astype(jnp.float32)
    for k in range(1, ranks):
        first += firsts_ref[k].astype(jnp.float32)
    first_out_ref[...] = first
    total = None
    for j in range(ranks):
        piece = pieces[0][own * points :, :]
        for r in range(1, ranks):
            piece = jnp.where(lax.rem(j + r, ranks) == me, pieces[r][own * points :, :], piece)
        piece = piece.astype(jnp.float32)
        total = piece if total is None else total + piece
    fold = share // LANES
    height = points // fold
    for q in range(own):
        for f in range(fold):
            second_out_ref[q, f * height : (f + 1) * height, :] = total[
                q * height : (q + 1) * height, f * LANES : (f + 1) * LANES
            ]


def shards(tokens, cotangent, kernel, first_factor, second_factor):
    ranks, members = lax.axis_size("dp"), lax.axis_size("seq")
    _, local_rows, channels = tokens.shape
    own, points, _ = second_factor.shape
    share = channels // ranks
    cols = share // LANES
    rows = 2 * cols * own
    groups = local_rows // own
    second_rows = own * points * members // share
    seq_share = 1.0 / math.sqrt(ranks)
    factor_share = 1.0 / math.sqrt(2.0 * channels * ranks)
    both = pl.BlockSpec((1, local_rows, share), lambda k: (0, 0, k))
    message = jax.ShapeDtypeStruct((ranks * members, rows, LANES), jnp.bfloat16)
    params = pltpu.CompilerParams(dimension_semantics=("arbitrary",), vmem_limit_bytes=32 * 1024 * 1024)
    wide = pltpu.CompilerParams(dimension_semantics=("arbitrary",), vmem_limit_bytes=58 * 1024 * 1024)
    row_scratch = pltpu.VMEM((groups * rows, LANES), jnp.float32)

    with jax.named_scope("mix"):
        mixed = pl.pallas_call(
            lambda *refs: mix_kernel(own, cols, *refs),
            out_shape=message,
            grid=(ranks,),
            in_specs=[pl.BlockSpec((1, local_rows, local_rows), lambda k: (0, 0, 0)), both, both],
            out_specs=pl.BlockSpec((members, rows, LANES), lambda k: (k, 0, 0)),
            scratch_shapes=[row_scratch, pltpu.VMEM((local_rows // LANES, local_rows, LANES), jnp.float32)],
            compiler_params=wide,
            name="mix",
        )(first_factor, tokens, cotangent)
    with jax.named_scope("send"):
        arrived = lax.all_to_all(mixed, ("dp", "seq"), split_axis=0, concat_axis=0, tiled=True)
    quarter = lax.dynamic_slice_in_dim(kernel, lax.axis_index("dp") * share, share, 1)
    with jax.named_scope("middle"):
        back, part = pl.pallas_call(
            lambda *refs: middle_kernel(own, cols, (seq_share, factor_share), *refs),
            out_shape=(
                jax.ShapeDtypeStruct((ranks, members, rows, LANES), jnp.bfloat16),
                jax.ShapeDtypeStruct((own * points + second_rows, share), jnp.bfloat16),
            ),
            grid=(ranks,),
            in_specs=[
                pl.BlockSpec((1, members, rows, LANES), lambda s: (s, 0, 0, 0)),
                pl.BlockSpec((own * points, share), lambda s: (0, 0)),
                pl.BlockSpec((own, points, members), lambda s: (0, 0, 0)),
            ],
            out_specs=(
                pl.BlockSpec((1, members, rows, LANES), lambda s: (s, 0, 0, 0)),
                pl.BlockSpec((own * points + second_rows, share), lambda s: (0, 0)),
            ),
            scratch_shapes=[
                row_scratch,
                pltpu.VMEM((own, points, share), jnp.float32),
                pltpu.VMEM((own, points, members), jnp.float32),
            ],
            compiler_params=params,
            name="middle",
        )(arrived.reshape(ranks, members, rows, LANES), quarter, second_factor)
    with jax.named_scope("gather_parts"):
        pieces = [part]
        for r in range(1, ranks):
            pieces.append(lax.ppermute(part, "dp", [(i, (i + r) % ranks) for i in range(ranks)]))
    with jax.named_scope("return"):
        returned = lax.all_to_all(
            back.reshape(ranks * members, rows, LANES), ("dp", "seq"), split_axis=0, concat_axis=0, tiled=True
        )
    with jax.named_scope("final"):
        whole = pl.BlockSpec(memory_space=pl.ANY)
        first_part = pl.pallas_call(
            lambda *refs: final_kernel(own, cols, ranks, factor_share, *refs),
            out_shape=jax.ShapeDtypeStruct((local_rows, local_rows), jnp.bfloat16),
            grid=(ranks,),
            in_specs=[pl.BlockSpec((members, rows, LANES), lambda k: (k, 0, 0)), whole, whole],
            out_specs=pl.BlockSpec((local_rows, local_rows), lambda k: (0, 0)),
            scratch_shapes=[
                row_scratch,
                pltpu.VMEM((local_rows // LANES, local_rows, LANES), jnp.float32),
                pltpu.VMEM((2, ranks, local_rows, share), jnp.bfloat16),
                pltpu.SemaphoreType.DMA((2, ranks)),
            ],
            compiler_params=pltpu.CompilerParams(
                dimension_semantics=("arbitrary",), vmem_limit_bytes=58 * 1024 * 1024
            ),
            name="final",
        )(returned, tokens, cotangent)
    with jax.named_scope("sum"):
        first_parts = lax.all_gather(first_part, "dp")
        kernel_out, first_out, second_out = pl.pallas_call(
            lambda *refs: join_kernel(ranks, *refs),
            out_shape=(
                jax.ShapeDtypeStruct((own * points, channels), jnp.bfloat16),
                jax.ShapeDtypeStruct((local_rows, local_rows), jnp.float32),
                jax.ShapeDtypeStruct((own, points, members), jnp.float32),
            ),
            compiler_params=pltpu.CompilerParams(vmem_limit_bytes=32 * 1024 * 1024),
            name="join",
        )(first_parts, *pieces)
    return kernel_out, first_out[None], second_out


def solution(mesh):
    in_specs = (
        P("dp", "seq", None),
        P("dp", "seq", None),
        P("seq", None),
        P("seq", None, None),
        P("seq", None, None),
    )
    out_specs = (P("seq", None), P("seq", None, None), P("seq", None, None))
    return jax.shard_map(shards, mesh=mesh, in_specs=in_specs, out_specs=out_specs, check_vma=False)
```

```python
import math

import jax
import jax.numpy as jnp
from jax import lax
from jax.experimental import pallas as pl
from jax.experimental.pallas import tpu as pltpu
from jax.sharding import PartitionSpec as P

LANES = 128


def nn(left, right):
    return lax.dot_general(left, right, (((1,), (0,)), ((), ())), preferred_element_type=jnp.float32)


def nt(left, right):
    return lax.dot_general(left, right, (((1,), (1,)), ((), ())), preferred_element_type=jnp.float32)


def tn(left, right):
    return lax.dot_general(left, right, (((0,), (0,)), ((), ())), preferred_element_type=jnp.float32)


def beside(rows, own, cols, q):
    return [
        jnp.concatenate([rows[(t * cols + ci) * own + q] for ci in range(cols)], axis=1) for t in range(2)
    ]


def mix_kernel(own, cols, first_ref, tokens_ref, cotangent_ref, out_ref, factor_ref):
    groups = out_ref.shape[0]

    @pl.when(pl.program_id(0) == 0)
    def _():
        for h in range(factor_ref.shape[0]):
            factor_ref[h] = first_ref[0, :, h * LANES : (h + 1) * LANES].astype(jnp.float32)

    pieces = [None] * out_ref.shape[1]
    for q in range(own):
        factor = jnp.concatenate(
            [
                factor_ref[h, pl.ds(q, groups, stride=own), :].astype(jnp.bfloat16)
                for h in range(factor_ref.shape[0])
            ],
            axis=1,
        )
        for t, ref in enumerate((tokens_ref, cotangent_ref)):
            mixed = nn(factor, ref[0]).astype(jnp.bfloat16)
            for ci in range(cols):
                pieces[(t * cols + ci) * own + q] = mixed[:, ci * LANES : (ci + 1) * LANES]
    out_ref[...] = jnp.swapaxes(jnp.stack(pieces), 0, 1)


def pack(blocks_ref, part_ref, start):
    own, points, _ = blocks_ref.shape
    fold = part_ref.shape[1] // LANES
    height = points // fold
    for q in range(own):
        for f in range(fold):
            part_ref[start + q * height : start + (q + 1) * height, f * LANES : (f + 1) * LANES] = blocks_ref[
                q, f * height : (f + 1) * height, :
            ].astype(jnp.bfloat16)


def middle_kernel(
    own, cols, shares, arrived_ref, kernel_ref, second_ref, back_ref, part_ref, total_ref, second_total_ref
):
    step = pl.program_id(0)
    last = pl.num_programs(0) - 1
    seq_share, factor_share = shares

    @pl.when(step == 0)
    def _():
        total_ref[...] = jnp.zeros_like(total_ref)
        second_total_ref[...] = jnp.zeros_like(second_total_ref)

    arrived = jnp.swapaxes(arrived_ref[0], 0, 1)
    pieces = [None] * arrived.shape[0]
    for q in range(own):
        factor = second_ref[q]
        mixed_in, mixed_up = beside(arrived, own, cols, q)
        forward = nn(factor, mixed_in)
        backward = nn(factor, mixed_up)
        points = factor.shape[0]
        scale = kernel_ref[q * points : (q + 1) * points, :].astype(jnp.float32)
        total_ref[q] += forward * backward
        weighted = (scale * forward).astype(jnp.bfloat16)
        pulled = (scale * backward).astype(jnp.bfloat16)
        second_total_ref[q] += (nt(pulled, mixed_in) + nt(weighted, mixed_up)) * factor_share
        for t, values in enumerate((weighted, pulled)):
            spread = tn(factor, values).astype(jnp.bfloat16)
            for ci in range(cols):
                pieces[(t * cols + ci) * own + q] = spread[:, ci * LANES : (ci + 1) * LANES]
    back_ref[0] = jnp.swapaxes(jnp.stack(pieces), 0, 1)

    @pl.when(step == last)
    def _():
        points = total_ref.shape[1]
        for q in range(own):
            part_ref[q * points : (q + 1) * points, :] = (total_ref[q] * seq_share).astype(jnp.bfloat16)
        pack(second_total_ref, part_ref, own * points)


def final_kernel(
    own, cols, ranks, factor_share, returned_ref, tokens_ref, cotangent_ref, out_ref, total_ref, rows_ref, held_ref, sems
):
    groups = returned_ref.shape[0]
    share = cols * LANES
    step = pl.program_id(0)
    last = pl.num_programs(0) - 1

    def loads(k):
        chunk = pl.ds(pl.multiple_of(k * share, share), share)
        return [
            pltpu.make_async_copy(ref.at[0, :, chunk], held_ref.at[t, k], sems.at[t, k])
            for t, ref in enumerate((tokens_ref, cotangent_ref))
        ]

    @pl.when(step == 0)
    def _():
        for k in range(ranks):
            for copy in loads(k):
                copy.start()
        total_ref[...] = jnp.zeros_like(total_ref)

    returned = jnp.swapaxes(returned_ref[...], 0, 1)
    for copy in loads(step):
        copy.wait()
    for q in range(own):
        spread, pulled_back = beside(returned, own, cols, q)
        total_ref[q] += nt(pulled_back, held_ref[0, step]) + nt(spread, held_ref[1, step])

    @pl.when(step == last)
    def _():
        for h in range(rows_ref.shape[0]):
            for q in range(own):
                rows_ref[h, pl.ds(q, groups, stride=own), :] = total_ref[q, :, h * LANES : (h + 1) * LANES]
            out_ref[:, h * LANES : (h + 1) * LANES] = (rows_ref[h] * factor_share).astype(jnp.bfloat16)


def join_kernel(ranks, firsts_ref, *refs):
    pieces, refs = refs[:ranks], refs[ranks:]
    kernel_out_ref, first_out_ref, second_out_ref, tails_ref, sems = refs
    own, points, _ = second_out_ref.shape
    _, tail_rows, share = tails_ref.shape
    me = lax.axis_index("dp")
    copies = []
    for r in range(ranks):
        sender = lax.rem(me + ranks - r, ranks)
        chunk = pl.ds(pl.multiple_of(sender * share, share), share)
        copies.append(
            (
                pltpu.make_async_copy(
                    pieces[r].at[pl.ds(0, own * points), :], kernel_out_ref.at[:, chunk], sems.at[0, r]
                ),
                pltpu.make_async_copy(
                    pieces[r].at[pl.ds(own * points, tail_rows), :], tails_ref.at[sender], sems.at[1, r]
                ),
            )
        )
    for pair in copies:
        for copy in pair:
            copy.start()
    first = firsts_ref[0].astype(jnp.float32)
    for k in range(1, ranks):
        first += firsts_ref[k].astype(jnp.float32)
    first_out_ref[...] = first
    for pair in copies:
        pair[1].wait()
    total = tails_ref[0].astype(jnp.float32)
    for k in range(1, ranks):
        total += tails_ref[k].astype(jnp.float32)
    fold = share // LANES
    height = points // fold
    for q in range(own):
        for f in range(fold):
            second_out_ref[q, f * height : (f + 1) * height, :] = total[
                q * height : (q + 1) * height, f * LANES : (f + 1) * LANES
            ]
    for pair in copies:
        pair[0].wait()


def in_hbm(array):
    return pltpu.with_memory_space_constraint(array, pltpu.HBM)


def shards(tokens, cotangent, kernel, first_factor, second_factor):
    ranks, members = lax.axis_size("dp"), lax.axis_size("seq")
    _, local_rows, channels = tokens.shape
    own, points, _ = second_factor.shape
    share = channels // ranks
    cols = share // LANES
    rows = 2 * cols * own
    groups = local_rows // own
    second_rows = own * points * members // share
    seq_share = 1.0 / math.sqrt(ranks)
    factor_share = 1.0 / math.sqrt(2.0 * channels * ranks)
    both = pl.BlockSpec((1, local_rows, share), lambda k: (0, 0, k))
    params = pltpu.CompilerParams(dimension_semantics=("arbitrary",), vmem_limit_bytes=32 * 1024 * 1024)

    with jax.named_scope("mix"):
        mixed = pl.pallas_call(
            lambda *refs: mix_kernel(own, cols, *refs),
            out_shape=pltpu.HBM((ranks * members, rows, LANES), jnp.bfloat16),
            grid=(ranks,),
            in_specs=[pl.BlockSpec((1, local_rows, local_rows), lambda k: (0, 0, 0)), both, both],
            out_specs=pl.BlockSpec((members, rows, LANES), lambda k: (k, 0, 0)),
            scratch_shapes=[pltpu.VMEM((local_rows // LANES, local_rows, LANES), jnp.float32)],
            compiler_params=params,
            name="mix",
        )(in_hbm(first_factor), in_hbm(tokens), in_hbm(cotangent))
    with jax.named_scope("send"):
        arrived = lax.all_to_all(mixed, ("dp", "seq"), split_axis=0, concat_axis=0, tiled=True)
    quarter = lax.dynamic_slice_in_dim(kernel, lax.axis_index("dp") * share, share, 1)
    with jax.named_scope("middle"):
        back, part = pl.pallas_call(
            lambda *refs: middle_kernel(own, cols, (seq_share, factor_share), *refs),
            out_shape=(
                pltpu.HBM((ranks, members, rows, LANES), jnp.bfloat16),
                pltpu.HBM((own * points + second_rows, share), jnp.bfloat16),
            ),
            grid=(ranks,),
            in_specs=[
                pl.BlockSpec((1, members, rows, LANES), lambda s: (s, 0, 0, 0)),
                pl.BlockSpec((own * points, share), lambda s: (0, 0)),
                pl.BlockSpec((own, points, members), lambda s: (0, 0, 0)),
            ],
            out_specs=(
                pl.BlockSpec((1, members, rows, LANES), lambda s: (s, 0, 0, 0)),
                pl.BlockSpec((own * points + second_rows, share), lambda s: (0, 0)),
            ),
            scratch_shapes=[
                pltpu.VMEM((own, points, share), jnp.float32),
                pltpu.VMEM((own, points, members), jnp.float32),
            ],
            compiler_params=params,
            name="middle",
        )(arrived.reshape(ranks, members, rows, LANES), quarter, second_factor)
    with jax.named_scope("gather_parts"):
        pieces = [part]
        for r in range(1, ranks):
            pieces.append(lax.ppermute(part, "dp", [(i, (i + r) % ranks) for i in range(ranks)]))
    with jax.named_scope("return"):
        returned = lax.all_to_all(
            back.reshape(ranks * members, rows, LANES), ("dp", "seq"), split_axis=0, concat_axis=0, tiled=True
        )
    with jax.named_scope("final"):
        whole = pl.BlockSpec(memory_space=pl.ANY)
        first_part = pl.pallas_call(
            lambda *refs: final_kernel(own, cols, ranks, factor_share, *refs),
            out_shape=jax.ShapeDtypeStruct((local_rows, local_rows), jnp.bfloat16),
            grid=(ranks,),
            in_specs=[pl.BlockSpec((members, rows, LANES), lambda k: (k, 0, 0)), whole, whole],
            out_specs=pl.BlockSpec((local_rows, local_rows), lambda k: (0, 0)),
            scratch_shapes=[
                pltpu.VMEM((own, groups, local_rows), jnp.float32),
                pltpu.VMEM((local_rows // LANES, local_rows, LANES), jnp.float32),
                pltpu.VMEM((2, ranks, local_rows, share), jnp.bfloat16),
                pltpu.SemaphoreType.DMA((2, ranks)),
            ],
            compiler_params=params,
            name="final",
        )(returned, in_hbm(tokens), in_hbm(cotangent))
    with jax.named_scope("sum"):
        first_parts = lax.all_gather(first_part, "dp")
        kernel_out, first_out, second_out = pl.pallas_call(
            lambda *refs: join_kernel(ranks, *refs),
            out_shape=(
                jax.ShapeDtypeStruct((own * points, channels), jnp.bfloat16),
                jax.ShapeDtypeStruct((local_rows, local_rows), jnp.float32),
                jax.ShapeDtypeStruct((own, points, members), jnp.float32),
            ),
            in_specs=[pl.BlockSpec(memory_space=pltpu.VMEM)] + [whole] * ranks,
            out_specs=(
                whole,
                pl.BlockSpec(memory_space=pltpu.VMEM),
                pl.BlockSpec(memory_space=pltpu.VMEM),
            ),
            scratch_shapes=[
                pltpu.VMEM((ranks, second_rows, share), jnp.bfloat16),
                pltpu.SemaphoreType.DMA((2, ranks)),
            ],
            compiler_params=pltpu.CompilerParams(vmem_limit_bytes=32 * 1024 * 1024),
            name="join",
        )(first_parts, *pieces)
    return kernel_out, first_out[None], second_out


def solution(mesh):
    in_specs = (
        P("dp", "seq", None),
        P("dp", "seq", None),
        P("seq", None),
        P("seq", None, None),
        P("seq", None, None),
    )
    out_specs = (P("seq", None), P("seq", None, None), P("seq", None, None))
    return jax.shard_map(shards, mesh=mesh, in_specs=in_specs, out_specs=out_specs, check_vma=False)
```

```python
import math

import jax
import jax.numpy as jnp
from jax import lax
from jax.experimental import pallas as pl
from jax.experimental.pallas import tpu as pltpu
from jax.sharding import PartitionSpec as P

LANES = 128


def nn(left, right):
    return lax.dot_general(left, right, (((1,), (0,)), ((), ())), preferred_element_type=jnp.float32)


def nt(left, right):
    return lax.dot_general(left, right, (((1,), (1,)), ((), ())), preferred_element_type=jnp.float32)


def tn(left, right):
    return lax.dot_general(left, right, (((0,), (0,)), ((), ())), preferred_element_type=jnp.float32)


def beside(rows, own, cols, q):
    return [
        jnp.concatenate([rows[(t * cols + ci) * own + q] for ci in range(cols)], axis=1) for t in range(2)
    ]


def mix_kernel(own, cols, first_ref, tokens_ref, cotangent_ref, out_ref, factor_ref):
    groups = out_ref.shape[0]

    @pl.when(pl.program_id(0) == 0)
    def _():
        for h in range(factor_ref.shape[0]):
            factor_ref[h] = first_ref[0, :, h * LANES : (h + 1) * LANES].astype(jnp.float32)

    pieces = [None] * out_ref.shape[1]
    for q in range(own):
        factor = jnp.concatenate(
            [
                factor_ref[h, pl.ds(q, groups, stride=own), :].astype(jnp.bfloat16)
                for h in range(factor_ref.shape[0])
            ],
            axis=1,
        )
        for t, ref in enumerate((tokens_ref, cotangent_ref)):
            mixed = nn(factor, ref[0]).astype(jnp.bfloat16)
            for ci in range(cols):
                pieces[(t * cols + ci) * own + q] = mixed[:, ci * LANES : (ci + 1) * LANES]
    out_ref[...] = jnp.swapaxes(jnp.stack(pieces), 0, 1)


def pack(blocks_ref, part_ref, start):
    own, points, _ = blocks_ref.shape
    fold = part_ref.shape[1] // LANES
    height = points // fold
    for q in range(own):
        for f in range(fold):
            part_ref[start + q * height : start + (q + 1) * height, f * LANES : (f + 1) * LANES] = blocks_ref[
                q, f * height : (f + 1) * height, :
            ].astype(jnp.bfloat16)


def middle_kernel(
    own, cols, shares, arrived_ref, kernel_ref, second_ref, back_ref, part_ref, total_ref, second_total_ref
):
    step = pl.program_id(0)
    last = pl.num_programs(0) - 1
    seq_share, factor_share = shares

    @pl.when(step == 0)
    def _():
        total_ref[...] = jnp.zeros_like(total_ref)
        second_total_ref[...] = jnp.zeros_like(second_total_ref)

    arrived = jnp.swapaxes(arrived_ref[0], 0, 1)
    pieces = [None] * arrived.shape[0]
    for q in range(own):
        factor = second_ref[q]
        mixed_in, mixed_up = beside(arrived, own, cols, q)
        forward = nn(factor, mixed_in)
        backward = nn(factor, mixed_up)
        points = factor.shape[0]
        scale = kernel_ref[q * points : (q + 1) * points, :].astype(jnp.float32)
        total_ref[q] += forward * backward
        weighted = (scale * forward).astype(jnp.bfloat16)
        pulled = (scale * backward).astype(jnp.bfloat16)
        second_total_ref[q] += (nt(pulled, mixed_in) + nt(weighted, mixed_up)) * factor_share
        for t, values in enumerate((weighted, pulled)):
            spread = tn(factor, values).astype(jnp.bfloat16)
            for ci in range(cols):
                pieces[(t * cols + ci) * own + q] = spread[:, ci * LANES : (ci + 1) * LANES]
    back_ref[0] = jnp.swapaxes(jnp.stack(pieces), 0, 1)

    @pl.when(step == last)
    def _():
        points = total_ref.shape[1]
        for q in range(own):
            part_ref[q * points : (q + 1) * points, :] = (total_ref[q] * seq_share).astype(jnp.bfloat16)
        pack(second_total_ref, part_ref, own * points)


def final_kernel(
    own, cols, ranks, factor_share, returned_ref, tokens_ref, cotangent_ref, out_ref, total_ref, rows_ref, held_ref, sems
):
    groups = returned_ref.shape[0]
    share = cols * LANES
    step = pl.program_id(0)
    last = pl.num_programs(0) - 1

    def loads(k):
        chunk = pl.ds(pl.multiple_of(k * share, share), share)
        return [
            pltpu.make_async_copy(ref.at[0, :, chunk], held_ref.at[t, k], sems.at[t, k])
            for t, ref in enumerate((tokens_ref, cotangent_ref))
        ]

    @pl.when(step == 0)
    def _():
        for k in range(ranks):
            for copy in loads(k):
                copy.start()
        total_ref[...] = jnp.zeros_like(total_ref)

    returned = jnp.swapaxes(returned_ref[...], 0, 1)
    for copy in loads(step):
        copy.wait()
    for q in range(own):
        spread, pulled_back = beside(returned, own, cols, q)
        total_ref[q] += nt(pulled_back, held_ref[0, step]) + nt(spread, held_ref[1, step])

    @pl.when(step == last)
    def _():
        for h in range(rows_ref.shape[0]):
            for q in range(own):
                rows_ref[h, pl.ds(q, groups, stride=own), :] = total_ref[q, :, h * LANES : (h + 1) * LANES]
            out_ref[:, h * LANES : (h + 1) * LANES] = (rows_ref[h] * factor_share).astype(jnp.bfloat16)


def join_kernel(ranks, firsts_ref, *refs):
    pieces, refs = refs[:ranks], refs[ranks:]
    kernel_out_ref, first_out_ref, second_out_ref, held_ref, tails_ref, load_sems, store_sems = refs
    own, points, _ = second_out_ref.shape
    _, tail_rows, share = tails_ref.shape
    me = lax.axis_index("dp")
    loads, tails, stores = [], [], []
    for r in range(ranks):
        sender = lax.rem(me + ranks - r, ranks)
        chunk = pl.ds(pl.multiple_of(sender * share, share), share)
        head = pl.ds(0, own * points)
        loads.append(pltpu.make_async_copy(pieces[r].at[head, :], held_ref.at[r], load_sems.at[0, r]))
        tails.append(
            pltpu.make_async_copy(
                pieces[r].at[pl.ds(own * points, tail_rows), :], tails_ref.at[sender], load_sems.at[1, r]
            )
        )
        stores.append(pltpu.make_async_copy(held_ref.at[r], kernel_out_ref.at[:, chunk], store_sems.at[r]))
    for copy in loads + tails:
        copy.start()
    for load, store in zip(loads, stores):
        load.wait()
        store.start()
    first = firsts_ref[0].astype(jnp.float32)
    for k in range(1, ranks):
        first += firsts_ref[k].astype(jnp.float32)
    first_out_ref[...] = first
    for copy in tails:
        copy.wait()
    total = tails_ref[0].astype(jnp.float32)
    for k in range(1, ranks):
        total += tails_ref[k].astype(jnp.float32)
    fold = share // LANES
    height = points // fold
    for q in range(own):
        for f in range(fold):
            second_out_ref[q, f * height : (f + 1) * height, :] = total[
                q * height : (q + 1) * height, f * LANES : (f + 1) * LANES
            ]
    for copy in stores:
        copy.wait()


def in_hbm(array):
    return pltpu.with_memory_space_constraint(array, pltpu.HBM)


def shards(tokens, cotangent, kernel, first_factor, second_factor):
    ranks, members = lax.axis_size("dp"), lax.axis_size("seq")
    _, local_rows, channels = tokens.shape
    own, points, _ = second_factor.shape
    share = channels // ranks
    cols = share // LANES
    rows = 2 * cols * own
    groups = local_rows // own
    second_rows = own * points * members // share
    seq_share = 1.0 / math.sqrt(ranks)
    factor_share = 1.0 / math.sqrt(2.0 * channels * ranks)
    both = pl.BlockSpec((1, local_rows, share), lambda k: (0, 0, k))
    params = pltpu.CompilerParams(dimension_semantics=("arbitrary",), vmem_limit_bytes=32 * 1024 * 1024)

    with jax.named_scope("mix"):
        mixed = pl.pallas_call(
            lambda *refs: mix_kernel(own, cols, *refs),
            out_shape=pltpu.HBM((ranks * members, rows, LANES), jnp.bfloat16),
            grid=(ranks,),
            in_specs=[pl.BlockSpec((1, local_rows, local_rows), lambda k: (0, 0, 0)), both, both],
            out_specs=pl.BlockSpec((members, rows, LANES), lambda k: (k, 0, 0)),
            scratch_shapes=[pltpu.VMEM((local_rows // LANES, local_rows, LANES), jnp.float32)],
            compiler_params=params,
            name="mix",
        )(in_hbm(first_factor), in_hbm(tokens), in_hbm(cotangent))
    with jax.named_scope("send"):
        arrived = lax.all_to_all(mixed, ("dp", "seq"), split_axis=0, concat_axis=0, tiled=True)
    quarter = lax.dynamic_slice_in_dim(kernel, lax.axis_index("dp") * share, share, 1)
    with jax.named_scope("middle"):
        back, part = pl.pallas_call(
            lambda *refs: middle_kernel(own, cols, (seq_share, factor_share), *refs),
            out_shape=(
                pltpu.HBM((ranks, members, rows, LANES), jnp.bfloat16),
                pltpu.HBM((own * points + second_rows, share), jnp.bfloat16),
            ),
            grid=(ranks,),
            in_specs=[
                pl.BlockSpec((1, members, rows, LANES), lambda s: (s, 0, 0, 0)),
                pl.BlockSpec((own * points, share), lambda s: (0, 0)),
                pl.BlockSpec((own, points, members), lambda s: (0, 0, 0)),
            ],
            out_specs=(
                pl.BlockSpec((1, members, rows, LANES), lambda s: (s, 0, 0, 0)),
                pl.BlockSpec((own * points + second_rows, share), lambda s: (0, 0)),
            ),
            scratch_shapes=[
                pltpu.VMEM((own, points, share), jnp.float32),
                pltpu.VMEM((own, points, members), jnp.float32),
            ],
            compiler_params=params,
            name="middle",
        )(arrived.reshape(ranks, members, rows, LANES), quarter, second_factor)
    with jax.named_scope("gather_parts"):
        pieces = [part]
        for r in range(1, ranks):
            pieces.append(lax.ppermute(part, "dp", [(i, (i + r) % ranks) for i in range(ranks)]))
    with jax.named_scope("return"):
        returned = lax.all_to_all(
            back.reshape(ranks * members, rows, LANES), ("dp", "seq"), split_axis=0, concat_axis=0, tiled=True
        )
    with jax.named_scope("final"):
        whole = pl.BlockSpec(memory_space=pl.ANY)
        first_part = pl.pallas_call(
            lambda *refs: final_kernel(own, cols, ranks, factor_share, *refs),
            out_shape=jax.ShapeDtypeStruct((local_rows, local_rows), jnp.bfloat16),
            grid=(ranks,),
            in_specs=[pl.BlockSpec((members, rows, LANES), lambda k: (k, 0, 0)), whole, whole],
            out_specs=pl.BlockSpec((local_rows, local_rows), lambda k: (0, 0)),
            scratch_shapes=[
                pltpu.VMEM((own, groups, local_rows), jnp.float32),
                pltpu.VMEM((local_rows // LANES, local_rows, LANES), jnp.float32),
                pltpu.VMEM((2, ranks, local_rows, share), jnp.bfloat16),
                pltpu.SemaphoreType.DMA((2, ranks)),
            ],
            compiler_params=params,
            name="final",
        )(returned, in_hbm(tokens), in_hbm(cotangent))
    with jax.named_scope("sum"):
        first_parts = lax.all_gather(first_part, "dp")
        kernel_out, first_out, second_out = pl.pallas_call(
            lambda *refs: join_kernel(ranks, *refs),
            out_shape=(
                jax.ShapeDtypeStruct((own * points, channels), jnp.bfloat16),
                jax.ShapeDtypeStruct((local_rows, local_rows), jnp.float32),
                jax.ShapeDtypeStruct((own, points, members), jnp.float32),
            ),
            in_specs=[pl.BlockSpec(memory_space=pltpu.VMEM)] + [whole] * ranks,
            out_specs=(
                whole,
                pl.BlockSpec(memory_space=pltpu.VMEM),
                pl.BlockSpec(memory_space=pltpu.VMEM),
            ),
            scratch_shapes=[
                pltpu.VMEM((ranks, own * points, share), jnp.bfloat16),
                pltpu.VMEM((ranks, second_rows, share), jnp.bfloat16),
                pltpu.SemaphoreType.DMA((2, ranks)),
                pltpu.SemaphoreType.DMA((ranks,)),
            ],
            compiler_params=pltpu.CompilerParams(vmem_limit_bytes=32 * 1024 * 1024),
            name="join",
        )(first_parts, *pieces)
    return kernel_out, first_out[None], second_out


def solution(mesh):
    in_specs = (
        P("dp", "seq", None),
        P("dp", "seq", None),
        P("seq", None),
        P("seq", None, None),
        P("seq", None, None),
    )
    out_specs = (P("seq", None), P("seq", None, None), P("seq", None, None))
    return jax.shard_map(shards, mesh=mesh, in_specs=in_specs, out_specs=out_specs, check_vma=False)
```

```python
import math

import jax
import jax.numpy as jnp
from jax import lax
from jax.experimental import pallas as pl
from jax.experimental.pallas import tpu as pltpu
from jax.sharding import PartitionSpec as P

LANES = 128


def nn(left, right):
    return lax.dot_general(left, right, (((1,), (0,)), ((), ())), preferred_element_type=jnp.float32)


def nt(left, right):
    return lax.dot_general(left, right, (((1,), (1,)), ((), ())), preferred_element_type=jnp.float32)


def tn(left, right):
    return lax.dot_general(left, right, (((0,), (0,)), ((), ())), preferred_element_type=jnp.float32)


def beside(rows, own, cols, q):
    return [
        jnp.concatenate([rows[(t * cols + ci) * own + q] for ci in range(cols)], axis=1) for t in range(2)
    ]


def mix_kernel(own, cols, first_ref, tokens_ref, cotangent_ref, out_ref, factor_ref):
    groups = out_ref.shape[0]

    @pl.when(pl.program_id(0) == 0)
    def _():
        for h in range(factor_ref.shape[0]):
            factor_ref[h] = first_ref[0, :, h * LANES : (h + 1) * LANES].astype(jnp.float32)

    pieces = [None] * out_ref.shape[1]
    for q in range(own):
        factor = jnp.concatenate(
            [
                factor_ref[h, pl.ds(q, groups, stride=own), :].astype(jnp.bfloat16)
                for h in range(factor_ref.shape[0])
            ],
            axis=1,
        )
        for t, ref in enumerate((tokens_ref, cotangent_ref)):
            mixed = nn(factor, ref[0]).astype(jnp.bfloat16)
            for ci in range(cols):
                pieces[(t * cols + ci) * own + q] = mixed[:, ci * LANES : (ci + 1) * LANES]
    out_ref[...] = jnp.swapaxes(jnp.stack(pieces), 0, 1)


def middle_kernel(
    own, cols, shares, arrived_ref, kernel_ref, second_ref, back_ref, part_ref, second_out_ref, total_ref, second_total_ref
):
    step = pl.program_id(0)
    last = pl.num_programs(0) - 1
    seq_share, factor_share = shares

    @pl.when(step == 0)
    def _():
        total_ref[...] = jnp.zeros_like(total_ref)
        second_total_ref[...] = jnp.zeros_like(second_total_ref)

    arrived = jnp.swapaxes(arrived_ref[0], 0, 1)
    pieces = [None] * arrived.shape[0]
    for q in range(own):
        factor = second_ref[q]
        mixed_in, mixed_up = beside(arrived, own, cols, q)
        forward = nn(factor, mixed_in)
        backward = nn(factor, mixed_up)
        points = factor.shape[0]
        scale = kernel_ref[q * points : (q + 1) * points, :].astype(jnp.float32)
        total_ref[q] += forward * backward
        weighted = (scale * forward).astype(jnp.bfloat16)
        pulled = (scale * backward).astype(jnp.bfloat16)
        second_total_ref[q] += (nt(pulled, mixed_in) + nt(weighted, mixed_up)) * factor_share
        for t, values in enumerate((weighted, pulled)):
            spread = tn(factor, values).astype(jnp.bfloat16)
            for ci in range(cols):
                pieces[(t * cols + ci) * own + q] = spread[:, ci * LANES : (ci + 1) * LANES]
    back_ref[0] = jnp.swapaxes(jnp.stack(pieces), 0, 1)

    @pl.when(step == last)
    def _():
        points, members = second_total_ref.shape[1:]
        for q in range(own):
            part_ref[q * points : (q + 1) * points, :] = (total_ref[q] * seq_share).astype(jnp.bfloat16)
            second_out_ref[:, q * members : (q + 1) * members] = second_total_ref[q].astype(jnp.bfloat16)


def final_kernel(
    own, cols, ranks, factor_share, returned_ref, second_ref, tokens_ref, cotangent_ref, out_ref, total_ref, rows_ref, held_ref, sems
):
    groups = returned_ref.shape[0]
    share = cols * LANES
    step = pl.program_id(0)
    last = pl.num_programs(0) - 1

    def loads(k):
        chunk = pl.ds(pl.multiple_of(k * share, share), share)
        return [
            pltpu.make_async_copy(ref.at[0, :, chunk], held_ref.at[t, k], sems.at[t, k])
            for t, ref in enumerate((tokens_ref, cotangent_ref))
        ]

    @pl.when(step == 0)
    def _():
        for k in range(ranks):
            for copy in loads(k):
                copy.start()
        total_ref[...] = jnp.zeros_like(total_ref)

    returned = jnp.swapaxes(returned_ref[...], 0, 1)
    for copy in loads(step):
        copy.wait()
    for q in range(own):
        spread, pulled_back = beside(returned, own, cols, q)
        total_ref[q] += nt(pulled_back, held_ref[0, step]) + nt(spread, held_ref[1, step])

    @pl.when(step == last)
    def _():
        height = rows_ref.shape[1]
        out_ref[height:, :] = second_ref[...]
        for h in range(rows_ref.shape[0]):
            for q in range(own):
                rows_ref[h, pl.ds(q, groups, stride=own), :] = total_ref[q, :, h * LANES : (h + 1) * LANES]
            out_ref[:height, h * LANES : (h + 1) * LANES] = (rows_ref[h] * factor_share).astype(jnp.bfloat16)


def join_kernel(ranks, gathered_ref, *refs):
    pieces, refs = refs[:ranks], refs[ranks:]
    kernel_out_ref, first_out_ref, second_out_ref, held_ref, load_sems, store_sems = refs
    own, points, members = second_out_ref.shape
    height = first_out_ref.shape[0]
    share = held_ref.shape[2]
    me = lax.axis_index("dp")
    loads, stores = [], []
    for r in range(ranks):
        chunk = pl.ds(pl.multiple_of(lax.rem(me + ranks - r, ranks) * share, share), share)
        loads.append(pltpu.make_async_copy(pieces[r], held_ref.at[r], load_sems.at[r]))
        stores.append(pltpu.make_async_copy(held_ref.at[r], kernel_out_ref.at[:, chunk], store_sems.at[r]))
    for copy in loads:
        copy.start()
    for load, store in zip(loads, stores):
        load.wait()
        store.start()
    total = gathered_ref[0].astype(jnp.float32)
    for k in range(1, ranks):
        total += gathered_ref[k].astype(jnp.float32)
    first_out_ref[...] = total[:height]
    for q in range(own):
        second_out_ref[q] = total[height:, q * members : (q + 1) * members]
    for copy in stores:
        copy.wait()


def in_hbm(array):
    return pltpu.with_memory_space_constraint(array, pltpu.HBM)


def shards(tokens, cotangent, kernel, first_factor, second_factor):
    ranks, members = lax.axis_size("dp"), lax.axis_size("seq")
    _, local_rows, channels = tokens.shape
    own, points, _ = second_factor.shape
    share = channels // ranks
    cols = share // LANES
    rows = 2 * cols * own
    groups = local_rows // own
    seq_share = 1.0 / math.sqrt(ranks)
    factor_share = 1.0 / math.sqrt(2.0 * channels * ranks)
    both = pl.BlockSpec((1, local_rows, share), lambda k: (0, 0, k))
    params = pltpu.CompilerParams(dimension_semantics=("arbitrary",), vmem_limit_bytes=32 * 1024 * 1024)

    with jax.named_scope("mix"):
        mixed = pl.pallas_call(
            lambda *refs: mix_kernel(own, cols, *refs),
            out_shape=pltpu.HBM((ranks * members, rows, LANES), jnp.bfloat16),
            grid=(ranks,),
            in_specs=[pl.BlockSpec((1, local_rows, local_rows), lambda k: (0, 0, 0)), both, both],
            out_specs=pl.BlockSpec((members, rows, LANES), lambda k: (k, 0, 0)),
            scratch_shapes=[pltpu.VMEM((local_rows // LANES, local_rows, LANES), jnp.float32)],
            compiler_params=params,
            name="mix",
        )(in_hbm(first_factor), in_hbm(tokens), in_hbm(cotangent))
    with jax.named_scope("send"):
        arrived = lax.all_to_all(mixed, ("dp", "seq"), split_axis=0, concat_axis=0, tiled=True)
    quarter = lax.dynamic_slice_in_dim(kernel, lax.axis_index("dp") * share, share, 1)
    with jax.named_scope("middle"):
        back, part, second_part = pl.pallas_call(
            lambda *refs: middle_kernel(own, cols, (seq_share, factor_share), *refs),
            out_shape=(
                pltpu.HBM((ranks, members, rows, LANES), jnp.bfloat16),
                pltpu.HBM((own * points, share), jnp.bfloat16),
                pltpu.HBM((points, own * members), jnp.bfloat16),
            ),
            grid=(ranks,),
            in_specs=[
                pl.BlockSpec((1, members, rows, LANES), lambda s: (s, 0, 0, 0)),
                pl.BlockSpec((own * points, share), lambda s: (0, 0)),
                pl.BlockSpec((own, points, members), lambda s: (0, 0, 0)),
            ],
            out_specs=(
                pl.BlockSpec((1, members, rows, LANES), lambda s: (s, 0, 0, 0)),
                pl.BlockSpec((own * points, share), lambda s: (0, 0)),
                pl.BlockSpec((points, own * members), lambda s: (0, 0)),
            ),
            scratch_shapes=[
                pltpu.VMEM((own, points, share), jnp.float32),
                pltpu.VMEM((own, points, members), jnp.float32),
            ],
            compiler_params=params,
            name="middle",
        )(arrived.reshape(ranks, members, rows, LANES), quarter, second_factor)
    with jax.named_scope("gather_parts"):
        pieces = [part]
        for r in range(1, ranks):
            pieces.append(lax.ppermute(part, "dp", [(i, (i + r) % ranks) for i in range(ranks)]))
    with jax.named_scope("return"):
        returned = lax.all_to_all(
            back.reshape(ranks * members, rows, LANES), ("dp", "seq"), split_axis=0, concat_axis=0, tiled=True
        )
    with jax.named_scope("final"):
        whole = pl.BlockSpec(memory_space=pl.ANY)
        factor_parts = pl.pallas_call(
            lambda *refs: final_kernel(own, cols, ranks, factor_share, *refs),
            out_shape=jax.ShapeDtypeStruct((local_rows + points, local_rows), jnp.bfloat16),
            grid=(ranks,),
            in_specs=[
                pl.BlockSpec((members, rows, LANES), lambda k: (k, 0, 0)),
                pl.BlockSpec((points, own * members), lambda k: (0, 0)),
                whole,
                whole,
            ],
            out_specs=pl.BlockSpec((local_rows + points, local_rows), lambda k: (0, 0)),
            scratch_shapes=[
                pltpu.VMEM((own, groups, local_rows), jnp.float32),
                pltpu.VMEM((local_rows // LANES, local_rows, LANES), jnp.float32),
                pltpu.VMEM((2, ranks, local_rows, share), jnp.bfloat16),
                pltpu.SemaphoreType.DMA((2, ranks)),
            ],
            compiler_params=params,
            name="final",
        )(returned, second_part, in_hbm(tokens), in_hbm(cotangent))
    with jax.named_scope("sum"):
        gathered = lax.all_gather(factor_parts, "dp")
        kernel_out, first_out, second_out = pl.pallas_call(
            lambda *refs: join_kernel(ranks, *refs),
            out_shape=(
                jax.ShapeDtypeStruct((own * points, channels), jnp.bfloat16),
                jax.ShapeDtypeStruct((local_rows, local_rows), jnp.float32),
                jax.ShapeDtypeStruct((own, points, members), jnp.float32),
            ),
            in_specs=[pl.BlockSpec(memory_space=pltpu.VMEM)] + [whole] * ranks,
            out_specs=(
                whole,
                pl.BlockSpec(memory_space=pltpu.VMEM),
                pl.BlockSpec(memory_space=pltpu.VMEM),
            ),
            scratch_shapes=[
                pltpu.VMEM((ranks, own * points, share), jnp.bfloat16),
                pltpu.SemaphoreType.DMA((ranks,)),
                pltpu.SemaphoreType.DMA((ranks,)),
            ],
            compiler_params=pltpu.CompilerParams(vmem_limit_bytes=32 * 1024 * 1024),
            name="join",
        )(gathered, *pieces)
    return kernel_out, first_out[None], second_out


def solution(mesh):
    in_specs = (
        P("dp", "seq", None),
        P("dp", "seq", None),
        P("seq", None),
        P("seq", None, None),
        P("seq", None, None),
    )
    out_specs = (P("seq", None), P("seq", None, None), P("seq", None, None))
    return jax.shard_map(shards, mesh=mesh, in_specs=in_specs, out_specs=out_specs, check_vma=False)
```

```python
import math

import jax
import jax.numpy as jnp
from jax import lax
from jax.experimental import pallas as pl
from jax.experimental.pallas import tpu as pltpu
from jax.sharding import PartitionSpec as P

LANES = 128


def nn(left, right):
    return lax.dot_general(left, right, (((1,), (0,)), ((), ())), preferred_element_type=jnp.float32)


def nt(left, right):
    return lax.dot_general(left, right, (((1,), (1,)), ((), ())), preferred_element_type=jnp.float32)


def tn(left, right):
    return lax.dot_general(left, right, (((0,), (0,)), ((), ())), preferred_element_type=jnp.float32)


def beside(rows, own, cols, q):
    return [
        jnp.concatenate([rows[(t * cols + ci) * own + q] for ci in range(cols)], axis=1) for t in range(2)
    ]


def loads(refs, held_ref, sems, share, k):
    chunk = pl.ds(pl.multiple_of(k * share, share), share)
    return [
        pltpu.make_async_copy(ref.at[0, :, chunk], held_ref.at[t, k], sems.at[t, k]) for t, ref in enumerate(refs)
    ]


def mix_kernel(own, cols, ranks, first_ref, tokens_ref, cotangent_ref, out_ref, factor_ref, held_ref, sems):
    groups = out_ref.shape[0]
    step = pl.program_id(0)
    sources = (tokens_ref, cotangent_ref)

    @pl.when(step == 0)
    def _():
        for k in range(ranks):
            for copy in loads(sources, held_ref, sems, cols * LANES, k):
                copy.start()
        for h in range(factor_ref.shape[0]):
            factor_ref[h] = first_ref[0, :, h * LANES : (h + 1) * LANES].astype(jnp.float32)

    for copy in loads(sources, held_ref, sems, cols * LANES, step):
        copy.wait()
    pieces = [None] * out_ref.shape[1]
    for q in range(own):
        factor = jnp.concatenate(
            [
                factor_ref[h, pl.ds(q, groups, stride=own), :].astype(jnp.bfloat16)
                for h in range(factor_ref.shape[0])
            ],
            axis=1,
        )
        for t in range(2):
            mixed = nn(factor, held_ref[t, step]).astype(jnp.bfloat16)
            for ci in range(cols):
                pieces[(t * cols + ci) * own + q] = mixed[:, ci * LANES : (ci + 1) * LANES]
    out_ref[...] = jnp.swapaxes(jnp.stack(pieces), 0, 1)


def middle_kernel(
    own, cols, shares, arrived_ref, kernel_ref, second_ref, back_ref, part_ref, second_out_ref, total_ref, second_total_ref
):
    step = pl.program_id(0)
    last = pl.num_programs(0) - 1
    seq_share, factor_share = shares

    @pl.when(step == 0)
    def _():
        total_ref[...] = jnp.zeros_like(total_ref)
        second_total_ref[...] = jnp.zeros_like(second_total_ref)

    arrived = jnp.swapaxes(arrived_ref[step], 0, 1)
    pieces = [None] * arrived.shape[0]
    for q in range(own):
        factor = second_ref[q]
        mixed_in, mixed_up = beside(arrived, own, cols, q)
        forward = nn(factor, mixed_in)
        backward = nn(factor, mixed_up)
        points = factor.shape[0]
        scale = kernel_ref[q * points : (q + 1) * points, :].astype(jnp.float32)
        total_ref[q] += forward * backward
        weighted = (scale * forward).astype(jnp.bfloat16)
        pulled = (scale * backward).astype(jnp.bfloat16)
        second_total_ref[q] += (nt(pulled, mixed_in) + nt(weighted, mixed_up)) * factor_share
        for t, values in enumerate((weighted, pulled)):
            spread = tn(factor, values).astype(jnp.bfloat16)
            for ci in range(cols):
                pieces[(t * cols + ci) * own + q] = spread[:, ci * LANES : (ci + 1) * LANES]
    back_ref[0] = jnp.swapaxes(jnp.stack(pieces), 0, 1)

    @pl.when(step == last)
    def _():
        points, members = second_total_ref.shape[1:]
        for q in range(own):
            part_ref[q * points : (q + 1) * points, :] = (total_ref[q] * seq_share).astype(jnp.bfloat16)
            second_out_ref[:, q * members : (q + 1) * members] = second_total_ref[q].astype(jnp.bfloat16)


def final_kernel(
    own, cols, ranks, factor_share, returned_ref, second_ref, tokens_ref, cotangent_ref, out_ref, total_ref, rows_ref, held_ref, sems
):
    groups = returned_ref.shape[1]
    share = cols * LANES
    step = pl.program_id(0)
    last = pl.num_programs(0) - 1

    sources = (tokens_ref, cotangent_ref)

    @pl.when(step == 0)
    def _():
        for k in range(ranks):
            for copy in loads(sources, held_ref, sems, share, k):
                copy.start()
        total_ref[...] = jnp.zeros_like(total_ref)

    returned = jnp.swapaxes(returned_ref[step], 0, 1)
    for copy in loads(sources, held_ref, sems, share, step):
        copy.wait()
    for q in range(own):
        spread, pulled_back = beside(returned, own, cols, q)
        total_ref[q] += nt(pulled_back, held_ref[0, step]) + nt(spread, held_ref[1, step])

    @pl.when(step == last)
    def _():
        height = rows_ref.shape[1]
        out_ref[height:, :] = second_ref[...]
        for h in range(rows_ref.shape[0]):
            for q in range(own):
                rows_ref[h, pl.ds(q, groups, stride=own), :] = total_ref[q, :, h * LANES : (h + 1) * LANES]
            out_ref[:height, h * LANES : (h + 1) * LANES] = (rows_ref[h] * factor_share).astype(jnp.bfloat16)


def join_kernel(ranks, gathered_ref, *refs):
    pieces, refs = refs[:ranks], refs[ranks:]
    kernel_out_ref, first_out_ref, second_out_ref, held_ref, load_sems, store_sems = refs
    own, points, members = second_out_ref.shape
    height = first_out_ref.shape[0]
    share = held_ref.shape[2]
    me = lax.axis_index("dp")
    loads, stores = [], []
    for r in range(ranks):
        chunk = pl.ds(pl.multiple_of(lax.rem(me + ranks - r, ranks) * share, share), share)
        loads.append(pltpu.make_async_copy(pieces[r], held_ref.at[r], load_sems.at[r]))
        stores.append(pltpu.make_async_copy(held_ref.at[r], kernel_out_ref.at[:, chunk], store_sems.at[r]))
    for copy in loads:
        copy.start()
    for load, store in zip(loads, stores):
        load.wait()
        store.start()
    total = gathered_ref[0].astype(jnp.float32)
    for k in range(1, ranks):
        total += gathered_ref[k].astype(jnp.float32)
    first_out_ref[...] = total[:height]
    for q in range(own):
        second_out_ref[q] = total[height:, q * members : (q + 1) * members]
    for copy in stores:
        copy.wait()


def in_hbm(array):
    return pltpu.with_memory_space_constraint(array, pltpu.HBM)


def shards(tokens, cotangent, kernel, first_factor, second_factor):
    ranks, members = lax.axis_size("dp"), lax.axis_size("seq")
    _, local_rows, channels = tokens.shape
    own, points, _ = second_factor.shape
    share = channels // ranks
    cols = share // LANES
    rows = 2 * cols * own
    groups = local_rows // own
    seq_share = 1.0 / math.sqrt(ranks)
    factor_share = 1.0 / math.sqrt(2.0 * channels * ranks)
    whole = pl.BlockSpec(memory_space=pl.ANY)
    vmem = pl.BlockSpec(memory_space=pltpu.VMEM)
    params = pltpu.CompilerParams(dimension_semantics=("arbitrary",), vmem_limit_bytes=32 * 1024 * 1024)

    with jax.named_scope("mix"):
        mixed = pl.pallas_call(
            lambda *refs: mix_kernel(own, cols, ranks, *refs),
            out_shape=pltpu.HBM((ranks * members, rows, LANES), jnp.bfloat16),
            grid=(ranks,),
            in_specs=[pl.BlockSpec((1, local_rows, local_rows), lambda k: (0, 0, 0)), whole, whole],
            out_specs=pl.BlockSpec((members, rows, LANES), lambda k: (k, 0, 0)),
            scratch_shapes=[
                pltpu.VMEM((local_rows // LANES, local_rows, LANES), jnp.float32),
                pltpu.VMEM((2, ranks, local_rows, share), jnp.bfloat16),
                pltpu.SemaphoreType.DMA((2, ranks)),
            ],
            compiler_params=params,
            name="mix",
        )(in_hbm(first_factor), in_hbm(tokens), in_hbm(cotangent))
    with jax.named_scope("send"):
        arrived = lax.all_to_all(mixed, ("dp", "seq"), split_axis=0, concat_axis=0, tiled=True)
    quarter = lax.dynamic_slice_in_dim(kernel, lax.axis_index("dp") * share, share, 1)
    with jax.named_scope("middle"):
        back, part, second_part = pl.pallas_call(
            lambda *refs: middle_kernel(own, cols, (seq_share, factor_share), *refs),
            out_shape=(
                pltpu.HBM((ranks, members, rows, LANES), jnp.bfloat16),
                pltpu.HBM((own * points, share), jnp.bfloat16),
                pltpu.HBM((points, own * members), jnp.bfloat16),
            ),
            grid=(ranks,),
            in_specs=[vmem, vmem, vmem],
            out_specs=(
                pl.BlockSpec((1, members, rows, LANES), lambda s: (s, 0, 0, 0)),
                pl.BlockSpec((own * points, share), lambda s: (0, 0)),
                pl.BlockSpec((points, own * members), lambda s: (0, 0)),
            ),
            scratch_shapes=[
                pltpu.VMEM((own, points, share), jnp.float32),
                pltpu.VMEM((own, points, members), jnp.float32),
            ],
            compiler_params=params,
            name="middle",
        )(arrived.reshape(ranks, members, rows, LANES), quarter, second_factor)
    with jax.named_scope("gather_parts"):
        pieces = [part]
        for r in range(1, ranks):
            pieces.append(lax.ppermute(part, "dp", [(i, (i + r) % ranks) for i in range(ranks)]))
    with jax.named_scope("return"):
        returned = lax.all_to_all(
            back.reshape(ranks * members, rows, LANES), ("dp", "seq"), split_axis=0, concat_axis=0, tiled=True
        )
    with jax.named_scope("final"):
        factor_parts = pl.pallas_call(
            lambda *refs: final_kernel(own, cols, ranks, factor_share, *refs),
            out_shape=jax.ShapeDtypeStruct((local_rows + points, local_rows), jnp.bfloat16),
            grid=(ranks,),
            in_specs=[vmem, vmem, whole, whole],
            out_specs=pl.BlockSpec((local_rows + points, local_rows), lambda k: (0, 0)),
            scratch_shapes=[
                pltpu.VMEM((own, groups, local_rows), jnp.float32),
                pltpu.VMEM((local_rows // LANES, local_rows, LANES), jnp.float32),
                pltpu.VMEM((2, ranks, local_rows, share), jnp.bfloat16),
                pltpu.SemaphoreType.DMA((2, ranks)),
            ],
            compiler_params=params,
            name="final",
        )(returned.reshape(ranks, members, rows, LANES), second_part, in_hbm(tokens), in_hbm(cotangent))
    with jax.named_scope("sum"):
        gathered = lax.all_gather(factor_parts, "dp")
        kernel_out, first_out, second_out = pl.pallas_call(
            lambda *refs: join_kernel(ranks, *refs),
            out_shape=(
                jax.ShapeDtypeStruct((own * points, channels), jnp.bfloat16),
                jax.ShapeDtypeStruct((local_rows, local_rows), jnp.float32),
                jax.ShapeDtypeStruct((own, points, members), jnp.float32),
            ),
            in_specs=[vmem] + [whole] * ranks,
            out_specs=(
                whole,
                pl.BlockSpec(memory_space=pltpu.VMEM),
                pl.BlockSpec(memory_space=pltpu.VMEM),
            ),
            scratch_shapes=[
                pltpu.VMEM((ranks, own * points, share), jnp.bfloat16),
                pltpu.SemaphoreType.DMA((ranks,)),
                pltpu.SemaphoreType.DMA((ranks,)),
            ],
            compiler_params=pltpu.CompilerParams(vmem_limit_bytes=32 * 1024 * 1024),
            name="join",
        )(gathered, *pieces)
    return kernel_out, first_out[None], second_out


def solution(mesh):
    in_specs = (
        P("dp", "seq", None),
        P("dp", "seq", None),
        P("seq", None),
        P("seq", None, None),
        P("seq", None, None),
    )
    out_specs = (P("seq", None), P("seq", None, None), P("seq", None, None))
    return jax.shard_map(shards, mesh=mesh, in_specs=in_specs, out_specs=out_specs, check_vma=False)
```

```python
import math

import jax
import jax.numpy as jnp
from jax import lax
from jax.experimental import pallas as pl
from jax.experimental.pallas import tpu as pltpu
from jax.sharding import PartitionSpec as P

LANES = 128


def nn(left, right):
    return lax.dot_general(left, right, (((1,), (0,)), ((), ())), preferred_element_type=jnp.float32)


def nt(left, right):
    return lax.dot_general(left, right, (((1,), (1,)), ((), ())), preferred_element_type=jnp.float32)


def tn(left, right):
    return lax.dot_general(left, right, (((0,), (0,)), ((), ())), preferred_element_type=jnp.float32)


def beside(rows, own, cols, q):
    return [
        jnp.concatenate([rows[(t * cols + ci) * own + q] for ci in range(cols)], axis=1) for t in range(2)
    ]


def loads(refs, held_ref, sems, share, k):
    chunk = pl.ds(pl.multiple_of(k * share, share), share)
    return [
        pltpu.make_async_copy(ref.at[0, :, chunk], held_ref.at[t, k], sems.at[t, k]) for t, ref in enumerate(refs)
    ]


def mix_kernel(own, cols, ranks, first_ref, tokens_ref, cotangent_ref, out_ref, factor_ref, held_ref, sems):
    groups = out_ref.shape[0]
    step = pl.program_id(0)
    sources = (tokens_ref, cotangent_ref)

    @pl.when(step == 0)
    def _():
        for k in range(ranks):
            for copy in loads(sources, held_ref, sems, cols * LANES, k):
                copy.start()
        for h in range(factor_ref.shape[0]):
            factor_ref[h] = first_ref[0, :, h * LANES : (h + 1) * LANES].astype(jnp.float32)

    for copy in loads(sources, held_ref, sems, cols * LANES, step):
        copy.wait()
    pieces = [None] * out_ref.shape[1]
    for q in range(own):
        factor = jnp.concatenate(
            [
                factor_ref[h, pl.ds(q, groups, stride=own), :].astype(jnp.bfloat16)
                for h in range(factor_ref.shape[0])
            ],
            axis=1,
        )
        for t in range(2):
            mixed = nn(factor, held_ref[t, step]).astype(jnp.bfloat16)
            for ci in range(cols):
                pieces[(t * cols + ci) * own + q] = mixed[:, ci * LANES : (ci + 1) * LANES]
    out_ref[...] = jnp.swapaxes(jnp.stack(pieces), 0, 1)


def products(own, cols, arrived_ref, kernel_ref, second_ref, step):
    arrived = jnp.swapaxes(arrived_ref[step], 0, 1)
    for q in range(own):
        factor = second_ref[q]
        mixed_in, mixed_up = beside(arrived, own, cols, q)
        forward = nn(factor, mixed_in)
        backward = nn(factor, mixed_up)
        points = factor.shape[0]
        scale = kernel_ref[q * points : (q + 1) * points, :].astype(jnp.float32)
        weighted = (scale * forward).astype(jnp.bfloat16)
        pulled = (scale * backward).astype(jnp.bfloat16)
        yield q, factor, (mixed_in, mixed_up), (forward, backward), (weighted, pulled)


def middle_kernel(own, cols, arrived_ref, kernel_ref, second_ref, back_ref):
    pieces = [None] * back_ref.shape[2]
    for q, factor, _, _, scaled in products(own, cols, arrived_ref, kernel_ref, second_ref, pl.program_id(0)):
        for t, values in enumerate(scaled):
            spread = tn(factor, values).astype(jnp.bfloat16)
            for ci in range(cols):
                pieces[(t * cols + ci) * own + q] = spread[:, ci * LANES : (ci + 1) * LANES]
    back_ref[0] = jnp.swapaxes(jnp.stack(pieces), 0, 1)


def gradients_kernel(
    own, cols, shares, arrived_ref, kernel_ref, second_ref, part_ref, second_out_ref, total_ref, second_total_ref
):
    step = pl.program_id(0)
    last = pl.num_programs(0) - 1
    seq_share, factor_share = shares

    @pl.when(step == 0)
    def _():
        total_ref[...] = jnp.zeros_like(total_ref)
        second_total_ref[...] = jnp.zeros_like(second_total_ref)

    for q, _, mixed, parts, scaled in products(own, cols, arrived_ref, kernel_ref, second_ref, 0):
        total_ref[q] += parts[0] * parts[1]
        second_total_ref[q] += (nt(scaled[1], mixed[0]) + nt(scaled[0], mixed[1])) * factor_share

    @pl.when(step == last)
    def _():
        points, members = second_total_ref.shape[1:]
        for q in range(own):
            part_ref[q * points : (q + 1) * points, :] = (total_ref[q] * seq_share).astype(jnp.bfloat16)
            second_out_ref[:, q * members : (q + 1) * members] = second_total_ref[q].astype(jnp.bfloat16)


def final_kernel(
    own, cols, ranks, factor_share, returned_ref, second_ref, tokens_ref, cotangent_ref, out_ref, total_ref, rows_ref, held_ref, sems
):
    groups = returned_ref.shape[1]
    share = cols * LANES
    step = pl.program_id(0)
    last = pl.num_programs(0) - 1

    sources = (tokens_ref, cotangent_ref)

    @pl.when(step == 0)
    def _():
        for k in range(ranks):
            for copy in loads(sources, held_ref, sems, share, k):
                copy.start()
        total_ref[...] = jnp.zeros_like(total_ref)

    returned = jnp.swapaxes(returned_ref[step], 0, 1)
    for copy in loads(sources, held_ref, sems, share, step):
        copy.wait()
    for q in range(own):
        spread, pulled_back = beside(returned, own, cols, q)
        total_ref[q] += nt(pulled_back, held_ref[0, step]) + nt(spread, held_ref[1, step])

    @pl.when(step == last)
    def _():
        height = rows_ref.shape[1]
        out_ref[height:, :] = second_ref[...]
        for h in range(rows_ref.shape[0]):
            for q in range(own):
                rows_ref[h, pl.ds(q, groups, stride=own), :] = total_ref[q, :, h * LANES : (h + 1) * LANES]
            out_ref[:height, h * LANES : (h + 1) * LANES] = (rows_ref[h] * factor_share).astype(jnp.bfloat16)


def join_kernel(ranks, gathered_ref, *refs):
    pieces, refs = refs[:ranks], refs[ranks:]
    kernel_out_ref, first_out_ref, second_out_ref, held_ref, load_sems, store_sems = refs
    own, points, members = second_out_ref.shape
    height = first_out_ref.shape[0]
    share = held_ref.shape[2]
    me = lax.axis_index("dp")
    loads, stores = [], []
    for r in range(ranks):
        chunk = pl.ds(pl.multiple_of(lax.rem(me + ranks - r, ranks) * share, share), share)
        loads.append(pltpu.make_async_copy(pieces[r], held_ref.at[r], load_sems.at[r]))
        stores.append(pltpu.make_async_copy(held_ref.at[r], kernel_out_ref.at[:, chunk], store_sems.at[r]))
    for copy in loads:
        copy.start()
    for load, store in zip(loads, stores):
        load.wait()
        store.start()
    total = gathered_ref[0].astype(jnp.float32)
    for k in range(1, ranks):
        total += gathered_ref[k].astype(jnp.float32)
    first_out_ref[...] = total[:height]
    for q in range(own):
        second_out_ref[q] = total[height:, q * members : (q + 1) * members]
    for copy in stores:
        copy.wait()


def in_hbm(array):
    return pltpu.with_memory_space_constraint(array, pltpu.HBM)


def shards(tokens, cotangent, kernel, first_factor, second_factor):
    ranks, members = lax.axis_size("dp"), lax.axis_size("seq")
    _, local_rows, channels = tokens.shape
    own, points, _ = second_factor.shape
    share = channels // ranks
    cols = share // LANES
    rows = 2 * cols * own
    groups = local_rows // own
    seq_share = 1.0 / math.sqrt(ranks)
    factor_share = 1.0 / math.sqrt(2.0 * channels * ranks)
    whole = pl.BlockSpec(memory_space=pl.ANY)
    vmem = pl.BlockSpec(memory_space=pltpu.VMEM)
    params = pltpu.CompilerParams(dimension_semantics=("arbitrary",), vmem_limit_bytes=32 * 1024 * 1024)

    with jax.named_scope("mix"):
        mixed = pl.pallas_call(
            lambda *refs: mix_kernel(own, cols, ranks, *refs),
            out_shape=pltpu.HBM((ranks * members, rows, LANES), jnp.bfloat16),
            grid=(ranks,),
            in_specs=[pl.BlockSpec((1, local_rows, local_rows), lambda k: (0, 0, 0)), whole, whole],
            out_specs=pl.BlockSpec((members, rows, LANES), lambda k: (k, 0, 0)),
            scratch_shapes=[
                pltpu.VMEM((local_rows // LANES, local_rows, LANES), jnp.float32),
                pltpu.VMEM((2, ranks, local_rows, share), jnp.bfloat16),
                pltpu.SemaphoreType.DMA((2, ranks)),
            ],
            compiler_params=params,
            name="mix",
        )(in_hbm(first_factor), in_hbm(tokens), in_hbm(cotangent))
    with jax.named_scope("send"):
        arrived = lax.all_to_all(mixed, ("dp", "seq"), split_axis=0, concat_axis=0, tiled=True)
    quarter = lax.dynamic_slice_in_dim(kernel, lax.axis_index("dp") * share, share, 1)
    held = (arrived.reshape(ranks, members, rows, LANES), quarter, second_factor)
    with jax.named_scope("middle"):
        back = pl.pallas_call(
            lambda *refs: middle_kernel(own, cols, *refs),
            out_shape=pltpu.HBM((ranks, members, rows, LANES), jnp.bfloat16),
            grid=(ranks,),
            in_specs=[vmem, vmem, vmem],
            out_specs=pl.BlockSpec((1, members, rows, LANES), lambda s: (s, 0, 0, 0)),
            compiler_params=params,
            name="middle",
        )(*held)
    with jax.named_scope("gradients"):
        part, second_part = pl.pallas_call(
            lambda *refs: gradients_kernel(own, cols, (seq_share, factor_share), *refs),
            out_shape=(
                jax.ShapeDtypeStruct((own * points, share), jnp.bfloat16),
                jax.ShapeDtypeStruct((points, own * members), jnp.bfloat16),
            ),
            grid=(ranks,),
            in_specs=[
                pl.BlockSpec((1, members, rows, LANES), lambda s: (s, 0, 0, 0)),
                pl.BlockSpec((own * points, share), lambda s: (0, 0)),
                pl.BlockSpec((own, points, members), lambda s: (0, 0, 0)),
            ],
            out_specs=(
                pl.BlockSpec((own * points, share), lambda s: (0, 0)),
                pl.BlockSpec((points, own * members), lambda s: (0, 0)),
            ),
            scratch_shapes=[
                pltpu.VMEM((own, points, share), jnp.float32),
                pltpu.VMEM((own, points, members), jnp.float32),
            ],
            compiler_params=pltpu.CompilerParams(
                dimension_semantics=("arbitrary",), vmem_limit_bytes=16 * 1024 * 1024
            ),
            name="gradients",
        )(in_hbm(held[0]), *held[1:])
    with jax.named_scope("gather_parts"):
        pieces = [in_hbm(part)]
        for r in range(1, ranks):
            pieces.append(lax.ppermute(part, "dp", [(i, (i + r) % ranks) for i in range(ranks)]))
    with jax.named_scope("return"):
        returned = lax.all_to_all(
            back.reshape(ranks * members, rows, LANES), ("dp", "seq"), split_axis=0, concat_axis=0, tiled=True
        )
    with jax.named_scope("final"):
        factor_parts = pl.pallas_call(
            lambda *refs: final_kernel(own, cols, ranks, factor_share, *refs),
            out_shape=jax.ShapeDtypeStruct((local_rows + points, local_rows), jnp.bfloat16),
            grid=(ranks,),
            in_specs=[vmem, vmem, whole, whole],
            out_specs=pl.BlockSpec((local_rows + points, local_rows), lambda k: (0, 0)),
            scratch_shapes=[
                pltpu.VMEM((own, groups, local_rows), jnp.float32),
                pltpu.VMEM((local_rows // LANES, local_rows, LANES), jnp.float32),
                pltpu.VMEM((2, ranks, local_rows, share), jnp.bfloat16),
                pltpu.SemaphoreType.DMA((2, ranks)),
            ],
            compiler_params=params,
            name="final",
        )(returned.reshape(ranks, members, rows, LANES), second_part, in_hbm(tokens), in_hbm(cotangent))
    with jax.named_scope("sum"):
        gathered = lax.all_gather(factor_parts, "dp")
        kernel_out, first_out, second_out = pl.pallas_call(
            lambda *refs: join_kernel(ranks, *refs),
            out_shape=(
                jax.ShapeDtypeStruct((own * points, channels), jnp.bfloat16),
                jax.ShapeDtypeStruct((local_rows, local_rows), jnp.float32),
                jax.ShapeDtypeStruct((own, points, members), jnp.float32),
            ),
            in_specs=[vmem] + [whole] * ranks,
            out_specs=(
                whole,
                pl.BlockSpec(memory_space=pltpu.VMEM),
                pl.BlockSpec(memory_space=pltpu.VMEM),
            ),
            scratch_shapes=[
                pltpu.VMEM((ranks, own * points, share), jnp.bfloat16),
                pltpu.SemaphoreType.DMA((ranks,)),
                pltpu.SemaphoreType.DMA((ranks,)),
            ],
            compiler_params=pltpu.CompilerParams(vmem_limit_bytes=32 * 1024 * 1024),
            name="join",
        )(gathered, *pieces)
    return kernel_out, first_out[None], second_out


def solution(mesh):
    in_specs = (
        P("dp", "seq", None),
        P("dp", "seq", None),
        P("seq", None),
        P("seq", None, None),
        P("seq", None, None),
    )
    out_specs = (P("seq", None), P("seq", None, None), P("seq", None, None))
    return jax.shard_map(shards, mesh=mesh, in_specs=in_specs, out_specs=out_specs, check_vma=False)
```

```python
import math

import jax
import jax.numpy as jnp
from jax import lax
from jax.experimental import pallas as pl
from jax.experimental.pallas import tpu as pltpu
from jax.sharding import PartitionSpec as P

LANES = 128


def nn(left, right):
    return lax.dot_general(left, right, (((1,), (0,)), ((), ())), preferred_element_type=jnp.float32)


def nt(left, right):
    return lax.dot_general(left, right, (((1,), (1,)), ((), ())), preferred_element_type=jnp.float32)


def tn(left, right):
    return lax.dot_general(left, right, (((0,), (0,)), ((), ())), preferred_element_type=jnp.float32)


def beside(rows, own, cols, q):
    return [
        jnp.concatenate([rows[(t * cols + ci) * own + q] for ci in range(cols)], axis=1) for t in range(2)
    ]


def loads(refs, held_ref, sems, share, k):
    chunk = pl.ds(pl.multiple_of(k * share, share), share)
    return [
        pltpu.make_async_copy(ref.at[0, :, chunk], held_ref.at[t, k], sems.at[t, k]) for t, ref in enumerate(refs)
    ]


def mix_kernel(
    own, cols, ranks, first_ref, tokens_ref, cotangent_ref, out_ref, raw_ref, factor_ref, held_ref, first_sem, sems
):
    groups = out_ref.shape[0]
    step = pl.program_id(0)
    sources = (tokens_ref, cotangent_ref)

    @pl.when(step == 0)
    def _():
        first = pltpu.make_async_copy(first_ref.at[0], raw_ref, first_sem)
        first.start()
        for k in range(ranks):
            for copy in loads(sources, held_ref, sems, cols * LANES, k):
                copy.start()
        first.wait()
        for h in range(factor_ref.shape[0]):
            factor_ref[h] = raw_ref[:, h * LANES : (h + 1) * LANES].astype(jnp.float32)

    for copy in loads(sources, held_ref, sems, cols * LANES, step):
        copy.wait()
    pieces = [None] * out_ref.shape[1]
    for q in range(own):
        factor = jnp.concatenate(
            [
                factor_ref[h, pl.ds(q, groups, stride=own), :].astype(jnp.bfloat16)
                for h in range(factor_ref.shape[0])
            ],
            axis=1,
        )
        for t in range(2):
            mixed = nn(factor, held_ref[t, step]).astype(jnp.bfloat16)
            for ci in range(cols):
                pieces[(t * cols + ci) * own + q] = mixed[:, ci * LANES : (ci + 1) * LANES]
    out_ref[...] = jnp.swapaxes(jnp.stack(pieces), 0, 1)


def products(own, cols, arrived_ref, kernel_ref, second_ref, step):
    arrived = jnp.swapaxes(arrived_ref[step], 0, 1)
    for q in range(own):
        factor = second_ref[q]
        mixed_in, mixed_up = beside(arrived, own, cols, q)
        forward = nn(factor, mixed_in)
        backward = nn(factor, mixed_up)
        points = factor.shape[0]
        scale = kernel_ref[q * points : (q + 1) * points, :].astype(jnp.float32)
        weighted = (scale * forward).astype(jnp.bfloat16)
        pulled = (scale * backward).astype(jnp.bfloat16)
        yield q, factor, (mixed_in, mixed_up), (forward, backward), (weighted, pulled)


def middle_kernel(own, cols, arrived_ref, kernel_ref, second_ref, back_ref):
    pieces = [None] * back_ref.shape[2]
    for q, factor, _, _, scaled in products(own, cols, arrived_ref, kernel_ref, second_ref, pl.program_id(0)):
        for t, values in enumerate(scaled):
            spread = tn(factor, values).astype(jnp.bfloat16)
            for ci in range(cols):
                pieces[(t * cols + ci) * own + q] = spread[:, ci * LANES : (ci + 1) * LANES]
    back_ref[0] = jnp.swapaxes(jnp.stack(pieces), 0, 1)


def gradients_kernel(
    own, cols, shares, arrived_ref, kernel_ref, second_ref, part_ref, second_out_ref, total_ref, second_total_ref
):
    step = pl.program_id(0)
    last = pl.num_programs(0) - 1
    seq_share, factor_share = shares

    @pl.when(step == 0)
    def _():
        total_ref[...] = jnp.zeros_like(total_ref)
        second_total_ref[...] = jnp.zeros_like(second_total_ref)

    for q, _, mixed, parts, scaled in products(own, cols, arrived_ref, kernel_ref, second_ref, 0):
        total_ref[q] += parts[0] * parts[1]
        second_total_ref[q] += (nt(scaled[1], mixed[0]) + nt(scaled[0], mixed[1])) * factor_share

    @pl.when(step == last)
    def _():
        points, members = second_total_ref.shape[1:]
        for q in range(own):
            part_ref[q * points : (q + 1) * points, :] = (total_ref[q] * seq_share).astype(jnp.bfloat16)
            second_out_ref[:, q * members : (q + 1) * members] = second_total_ref[q].astype(jnp.bfloat16)


def final_kernel(
    own, cols, ranks, factor_share, returned_ref, second_ref, tokens_ref, cotangent_ref, out_ref, total_ref, rows_ref, held_ref, sems
):
    groups = returned_ref.shape[1]
    share = cols * LANES
    step = pl.program_id(0)
    last = pl.num_programs(0) - 1

    sources = (tokens_ref, cotangent_ref)

    @pl.when(step == 0)
    def _():
        for k in range(ranks):
            for copy in loads(sources, held_ref, sems, share, k):
                copy.start()
        total_ref[...] = jnp.zeros_like(total_ref)

    returned = jnp.swapaxes(returned_ref[step], 0, 1)
    for copy in loads(sources, held_ref, sems, share, step):
        copy.wait()
    for q in range(own):
        spread, pulled_back = beside(returned, own, cols, q)
        total_ref[q] += nt(pulled_back, held_ref[0, step]) + nt(spread, held_ref[1, step])

    @pl.when(step == last)
    def _():
        height = rows_ref.shape[1]
        out_ref[height:, :] = second_ref[...]
        for h in range(rows_ref.shape[0]):
            for q in range(own):
                rows_ref[h, pl.ds(q, groups, stride=own), :] = total_ref[q, :, h * LANES : (h + 1) * LANES]
            out_ref[:height, h * LANES : (h + 1) * LANES] = (rows_ref[h] * factor_share).astype(jnp.bfloat16)


def join_kernel(ranks, gathered_ref, *refs):
    pieces, refs = refs[:ranks], refs[ranks:]
    kernel_out_ref, first_out_ref, second_out_ref, held_ref, load_sems, store_sems = refs
    own, points, members = second_out_ref.shape
    height = first_out_ref.shape[0]
    share = held_ref.shape[2]
    me = lax.axis_index("dp")
    loads, stores = [], []
    for r in range(ranks):
        chunk = pl.ds(pl.multiple_of(lax.rem(me + ranks - r, ranks) * share, share), share)
        loads.append(pltpu.make_async_copy(pieces[r], held_ref.at[r], load_sems.at[r]))
        stores.append(pltpu.make_async_copy(held_ref.at[r], kernel_out_ref.at[:, chunk], store_sems.at[r]))
    for copy in loads:
        copy.start()
    for load, store in zip(loads, stores):
        load.wait()
        store.start()
    total = gathered_ref[0].astype(jnp.float32)
    for k in range(1, ranks):
        total += gathered_ref[k].astype(jnp.float32)
    first_out_ref[...] = total[:height]
    for q in range(own):
        second_out_ref[q] = total[height:, q * members : (q + 1) * members]
    for copy in stores:
        copy.wait()


def in_hbm(array):
    return pltpu.with_memory_space_constraint(array, pltpu.HBM)


def shards(tokens, cotangent, kernel, first_factor, second_factor):
    ranks, members = lax.axis_size("dp"), lax.axis_size("seq")
    _, local_rows, channels = tokens.shape
    own, points, _ = second_factor.shape
    share = channels // ranks
    cols = share // LANES
    rows = 2 * cols * own
    groups = local_rows // own
    seq_share = 1.0 / math.sqrt(ranks)
    factor_share = 1.0 / math.sqrt(2.0 * channels * ranks)
    whole = pl.BlockSpec(memory_space=pl.ANY)
    vmem = pl.BlockSpec(memory_space=pltpu.VMEM)
    params = pltpu.CompilerParams(dimension_semantics=("arbitrary",), vmem_limit_bytes=32 * 1024 * 1024)

    with jax.named_scope("mix"):
        mixed = pl.pallas_call(
            lambda *refs: mix_kernel(own, cols, ranks, *refs),
            out_shape=pltpu.HBM((ranks * members, rows, LANES), jnp.bfloat16),
            grid=(ranks,),
            in_specs=[whole, whole, whole],
            out_specs=pl.BlockSpec((members, rows, LANES), lambda k: (k, 0, 0)),
            scratch_shapes=[
                pltpu.VMEM((local_rows, local_rows), jnp.bfloat16),
                pltpu.VMEM((local_rows // LANES, local_rows, LANES), jnp.float32),
                pltpu.VMEM((2, ranks, local_rows, share), jnp.bfloat16),
                pltpu.SemaphoreType.DMA(()),
                pltpu.SemaphoreType.DMA((2, ranks)),
            ],
            compiler_params=params,
            name="mix",
        )(in_hbm(first_factor), in_hbm(tokens), in_hbm(cotangent))
    with jax.named_scope("send"):
        arrived = lax.all_to_all(mixed, ("dp", "seq"), split_axis=0, concat_axis=0, tiled=True)
    quarter = lax.dynamic_slice_in_dim(kernel, lax.axis_index("dp") * share, share, 1)
    held = (arrived.reshape(ranks, members, rows, LANES), quarter, second_factor)
    with jax.named_scope("middle"):
        back = pl.pallas_call(
            lambda *refs: middle_kernel(own, cols, *refs),
            out_shape=pltpu.HBM((ranks, members, rows, LANES), jnp.bfloat16),
            grid=(ranks,),
            in_specs=[vmem, vmem, vmem],
            out_specs=pl.BlockSpec((1, members, rows, LANES), lambda s: (s, 0, 0, 0)),
            compiler_params=params,
            name="middle",
        )(*held)
    with jax.named_scope("gradients"):
        part, second_part = pl.pallas_call(
            lambda *refs: gradients_kernel(own, cols, (seq_share, factor_share), *refs),
            out_shape=(
                jax.ShapeDtypeStruct((own * points, share), jnp.bfloat16),
                jax.ShapeDtypeStruct((points, own * members), jnp.bfloat16),
            ),
            grid=(ranks,),
            in_specs=[
                pl.BlockSpec((1, members, rows, LANES), lambda s: (s, 0, 0, 0)),
                pl.BlockSpec((own * points, share), lambda s: (0, 0)),
                pl.BlockSpec((own, points, members), lambda s: (0, 0, 0)),
            ],
            out_specs=(
                pl.BlockSpec((own * points, share), lambda s: (0, 0)),
                pl.BlockSpec((points, own * members), lambda s: (0, 0)),
            ),
            scratch_shapes=[
                pltpu.VMEM((own, points, share), jnp.float32),
                pltpu.VMEM((own, points, members), jnp.float32),
            ],
            compiler_params=pltpu.CompilerParams(
                dimension_semantics=("arbitrary",), vmem_limit_bytes=16 * 1024 * 1024
            ),
            name="gradients",
        )(in_hbm(held[0]), *held[1:])
    with jax.named_scope("gather_parts"):
        pieces = [in_hbm(part)]
        for r in range(1, ranks):
            pieces.append(lax.ppermute(part, "dp", [(i, (i + r) % ranks) for i in range(ranks)]))
    with jax.named_scope("return"):
        returned = lax.all_to_all(
            back.reshape(ranks * members, rows, LANES), ("dp", "seq"), split_axis=0, concat_axis=0, tiled=True
        )
    with jax.named_scope("final"):
        factor_parts = pl.pallas_call(
            lambda *refs: final_kernel(own, cols, ranks, factor_share, *refs),
            out_shape=jax.ShapeDtypeStruct((local_rows + points, local_rows), jnp.bfloat16),
            grid=(ranks,),
            in_specs=[vmem, vmem, whole, whole],
            out_specs=pl.BlockSpec((local_rows + points, local_rows), lambda k: (0, 0)),
            scratch_shapes=[
                pltpu.VMEM((own, groups, local_rows), jnp.float32),
                pltpu.VMEM((local_rows // LANES, local_rows, LANES), jnp.float32),
                pltpu.VMEM((2, ranks, local_rows, share), jnp.bfloat16),
                pltpu.SemaphoreType.DMA((2, ranks)),
            ],
            compiler_params=params,
            name="final",
        )(returned.reshape(ranks, members, rows, LANES), second_part, in_hbm(tokens), in_hbm(cotangent))
    with jax.named_scope("sum"):
        gathered = lax.all_gather(factor_parts, "dp")
        kernel_out, first_out, second_out = pl.pallas_call(
            lambda *refs: join_kernel(ranks, *refs),
            out_shape=(
                jax.ShapeDtypeStruct((own * points, channels), jnp.bfloat16),
                jax.ShapeDtypeStruct((local_rows, local_rows), jnp.float32),
                jax.ShapeDtypeStruct((own, points, members), jnp.float32),
            ),
            in_specs=[vmem] + [whole] * ranks,
            out_specs=(
                whole,
                pl.BlockSpec(memory_space=pltpu.VMEM),
                pl.BlockSpec(memory_space=pltpu.VMEM),
            ),
            scratch_shapes=[
                pltpu.VMEM((ranks, own * points, share), jnp.bfloat16),
                pltpu.SemaphoreType.DMA((ranks,)),
                pltpu.SemaphoreType.DMA((ranks,)),
            ],
            compiler_params=pltpu.CompilerParams(vmem_limit_bytes=32 * 1024 * 1024),
            name="join",
        )(gathered, *pieces)
    return kernel_out, first_out[None], second_out


def solution(mesh):
    in_specs = (
        P("dp", "seq", None),
        P("dp", "seq", None),
        P("seq", None),
        P("seq", None, None),
        P("seq", None, None),
    )
    out_specs = (P("seq", None), P("seq", None, None), P("seq", None, None))
    return jax.shard_map(shards, mesh=mesh, in_specs=in_specs, out_specs=out_specs, check_vma=False)
```
